32 devices in a mesh: groups: 2 (over x), ctx: 16 (over z, y, core).
Axes of the slice: x: 2, y: 2, z: 4, core: 2. Of those that a mesh axis runs over, the one named last changes fastest.
Arguments:
- queries: bfloat16 [16384, 3584], P(('groups', 'ctx')), parts along dimension 0, may hold values from -48 to 48
- keys: bfloat16 [16384, 512], P(('groups', 'ctx')), parts along dimension 0, may hold values from -6 to 6
- values: bfloat16 [16384, 512], P(('groups', 'ctx')), parts along dimension 0, may hold values from -6 to 6
- out_grad: bfloat16 [16384, 3584], P(('groups', 'ctx')), parts along dimension 0, may hold values from -6 to 6
- links: int32 [128, 4], P(('groups', 'ctx')), parts along dimension 0, may hold values from -1 to 3, as said below
- header_blocks: int32 [8], P('groups'), parts along dimension 0, may hold values from 0 to 59, as said below
Outputs:
- query_grad: bfloat16 [16384, 3584], P(('groups', 'ctx')), parts along dimension 0
- key_gradient_array: float32 [16384, 512], P(('groups', 'ctx')), parts along dimension 0
- value_gradient_array: float32 [16384, 512], P(('groups', 'ctx')), parts along dimension 0
The draws below stay inside these ranges and needn't reach their ends.
There are 2 independent parts, one for each index of `groups`. The reference program is written for one: setup_inputs(seed, part) draws one part's arguments, and reference() takes and returns one part's arrays. A program takes and returns all parts, laid end to end along the dimension named above; each array names one. Nothing has to cross between parts.
Inputs may be any that keep to these rules, and one draw needn't show every extreme that they name: `header_blocks`: strictly increasing; no two header blocks lie among the same aligned 4 blocks, and none lies among the last 4 blocks. Non-empty entries of one row are distinct header numbers whose header block ends before the row's window part begins (header_blocks[links[b, l]] <= b - 256 / 128 - 1). The last row has no empty entry.
All inputs are finite; a program needn't handle non-finite values.
Results may differ from the reference program's by a relative error of at most 0.012.
Values may be sent and summed in bfloat16 or wider, within the bound.
No kernel may reach another device: no remote copies, remote signals or barrier semaphores. Data moves between devices by JAX's collectives and lax.ppermute only.
A program may use at most 192 MiB of HBM per device.

```python
import jax
import jax.numpy as jnp
from jax import lax

QUERY_HEADS = 28
KEY_VALUE_HEADS = 4
HEAD_SIZE = 128
BLK = 128
WIN = 256
LINKS = 4
BLK_DEV = 4
SEQUENCE_SPAN = 8192
NQB = 64
NH = 4


def query_key_pair(key):
    query_key = jax.random.fold_in(key, 11)
    key_lookup_name = jax.random.fold_in(key, 12)
    query_out = jnp.clip(jax.random.normal(query_key, (SEQUENCE_SPAN, QUERY_HEADS * HEAD_SIZE), jnp.float32), -6.0, 6.0)
    key_result_output = jnp.clip(jax.random.normal(key_lookup_name, (SEQUENCE_SPAN, KEY_VALUE_HEADS * HEAD_SIZE), jnp.float32), -6.0, 6.0)
    return (query_out, key_result_output)


def draw_queries(key, part):
    return query_key_pair(key)[0].astype(jnp.bfloat16)


def draw_keys(key, part):
    return query_key_pair(key)[1].astype(jnp.bfloat16)


def header_layout(key):
    base = jax.random.fold_in(key, 21)
    device_count = NQB // BLK_DEV
    middle = jax.random.permutation(jax.random.fold_in(base, 1), device_count - 3)[:NH - 2].astype(jnp.int32) + 1
    owners = jnp.sort(jnp.concatenate([jnp.zeros((1,), jnp.int32), middle, jnp.full((1,), device_count - 2, jnp.int32)]))
    offsets = jax.random.randint(jax.random.fold_in(base, 2), (NH,), 0, BLK_DEV).astype(jnp.int32)
    offsets = offsets.at[0].set(0).at[NH - 1].set(BLK_DEV - 1)
    return (owners * BLK_DEV + offsets).astype(jnp.int32)


def draw_header_blocks(key, part):
    return header_layout(key)


def draw_links(key, part):
    blocks = header_layout(key)
    base = jax.random.fold_in(key, 31)
    row_ids = jnp.arange(NQB, dtype=jnp.int32)
    slot_ids = jnp.arange(NH, dtype=jnp.int32)
    eligible = blocks[None, :] <= row_ids[:, None] - WIN // BLK - 1
    noise = jax.random.randint(jax.random.fold_in(base, 1), (NQB, NH), 0, 1 << 16).astype(jnp.int32)
    score = noise * NH + slot_ids[None, :]
    forced = (row_ids[:, None] == NQB - 1) & (slot_ids[None, :] == NH - 1)
    score = score + eligible.astype(jnp.int32) * (1 << 25) + forced.astype(jnp.int32) * (1 << 24)
    ignored, chosen = lax.top_k(score, LINKS)
    density = jax.random.randint(jax.random.fold_in(base, 2), (NQB // BLK_DEV,), 0, LINKS + 1).astype(jnp.int32)
    row_cap = jnp.repeat(density, BLK_DEV)
    counts = jax.random.randint(jax.random.fold_in(base, 3), (NQB,), 0, row_cap + 1).astype(jnp.int32)
    counts = jnp.where(row_ids == NQB - 1, LINKS, counts)
    usable = jnp.take_along_axis(eligible, chosen, axis=1)
    keep_entry = (jnp.arange(LINKS, dtype=jnp.int32)[None, :] < counts[:, None]) & usable
    return jnp.where(keep_entry, chosen, -1).astype(jnp.int32)


def levels(own_key, dims, split, low, high):
    factor_of, own = 1.0, jax.random.fold_in(own_key, 6)
    for axis_at, parts in split:
        draws = jnp.exp(jax.random.uniform(jax.random.fold_in(own, axis_at), (parts,), jnp.float32, low / len(split), high / len(split)))
        factor_of = factor_of * jnp.repeat(draws, dims[axis_at] // parts).reshape([-1 if axis == axis_at else 1 for axis in range(len(dims))])
    return factor_of


def centred(rng, extent, scale, limit, cuts=(), kind=jnp.bfloat16):
    values = scale * jax.random.normal(rng, extent, jnp.float32)
    if cuts:
        values = values * levels(rng, extent, cuts, -0.22, 0.18)
    return jnp.clip(values, -limit, limit).astype(kind)


def setup_inputs(seed: int = 0, part: int = 0) -> dict:
    key_list = jax.random.split(jax.random.key(seed), 7)
    part_splits = jax.random.split(jax.random.fold_in(key_list[6], part), 7)
    return {
        "queries": draw_queries(jax.random.fold_in(jax.random.fold_in(key_list[6], part), 71), part),
        "keys": draw_keys(jax.random.fold_in(jax.random.fold_in(key_list[6], part), 71), part),
        "values": centred(part_splits[2], (SEQUENCE_SPAN, KEY_VALUE_HEADS * HEAD_SIZE), 1.0, 6.0, ((0, 16),)),
        "out_grad": centred(part_splits[3], (SEQUENCE_SPAN, QUERY_HEADS * HEAD_SIZE), 1.0, 6.0, ((0, 16),)),
        "links": draw_links(jax.random.fold_in(jax.random.fold_in(key_list[6], part), 71), part),
        "header_blocks": draw_header_blocks(jax.random.fold_in(jax.random.fold_in(key_list[6], part), 71), part),
    }


def block_grads(query_row_block, gradient_row_block, key_row_block, value_row_block, is_valid):
    row_total_count = query_row_block.shape[0]
    key_total_count = key_row_block.shape[0]
    queries_each_group = QUERY_HEADS // KEY_VALUE_HEADS
    factor = float(HEAD_SIZE) ** -0.5
    highest = lax.Precision.HIGHEST
    query_four_axes = query_row_block.astype(jnp.float32).reshape(row_total_count, KEY_VALUE_HEADS, queries_each_group, HEAD_SIZE)
    gradient_four_axes = gradient_row_block.astype(jnp.float32).reshape(row_total_count, KEY_VALUE_HEADS, queries_each_group, HEAD_SIZE)
    key_three_axes = key_row_block.astype(jnp.float32).reshape(key_total_count, KEY_VALUE_HEADS, HEAD_SIZE)
    value_three_axes = value_row_block.astype(jnp.float32).reshape(key_total_count, KEY_VALUE_HEADS, HEAD_SIZE)
    scores = jnp.einsum("qgrd,kgd->gqrk", query_four_axes, key_three_axes, precision=highest) * factor
    scores = jnp.where(is_valid[None, :, None, :], scores, -1e30)
    row_max = jnp.max(scores, axis=-1, keepdims=True)
    weights = jnp.exp(scores - row_max)
    attend = weights / jnp.sum(weights, axis=-1, keepdims=True)
    d_attend = jnp.einsum("qgrd,kgd->gqrk", gradient_four_axes, value_three_axes, precision=highest)
    row_delta = jnp.sum(attend * d_attend, axis=-1, keepdims=True)
    d_scores = (attend * (d_attend - row_delta) * factor).astype(jnp.bfloat16).astype(jnp.float32)
    attend_low = attend.astype(jnp.bfloat16).astype(jnp.float32)
    query_grad = jnp.einsum("gqrk,kgd->qgrd", d_scores, key_three_axes, precision=highest)
    key_gradient_array = jnp.einsum("gqrk,qgrd->kgd", d_scores, query_four_axes, precision=highest)
    value_gradient_array = jnp.einsum("gqrk,qgrd->kgd", attend_low, gradient_four_axes, precision=highest)
    key_value_gradient = jnp.concatenate([key_gradient_array.reshape(key_total_count, KEY_VALUE_HEADS * HEAD_SIZE), value_gradient_array.reshape(key_total_count, KEY_VALUE_HEADS * HEAD_SIZE)], axis=1)
    return query_grad.reshape(row_total_count, QUERY_HEADS * HEAD_SIZE), key_value_gradient


def reference(queries, keys, values, out_grad, links, header_blocks):
    seq_len = queries.shape[0]
    block_total = seq_len // BLK
    half_width = keys.shape[1]
    kv_full = jnp.concatenate([keys, values], axis=1)
    kv_width = kv_full.shape[1]
    padded = jnp.concatenate([jnp.zeros((WIN, kv_width), kv_full.dtype), kv_full], axis=0)
    window_span = WIN + BLK

    def one_block(acc, block_id):
        row_start = (block_id * BLK).astype(jnp.int32)
        query_row_block = lax.dynamic_slice_in_dim(queries, row_start, BLK, 0)
        gradient_row_block = lax.dynamic_slice_in_dim(out_grad, row_start, BLK, 0)
        window = lax.dynamic_slice_in_dim(padded, row_start, window_span, 0)
        entries = links[block_id]
        is_live = entries >= 0
        safe_slot = jnp.where(is_live, entries, 0).astype(jnp.int32)
        header_ids = header_blocks[safe_slot].astype(jnp.int32)
        pieces = [lax.dynamic_slice_in_dim(kv_full, (header_ids[slot] * BLK).astype(jnp.int32), BLK, 0) for slot in range(LINKS)]
        key_tile = jnp.concatenate([window] + pieces, axis=0)
        q_pos = row_start + jnp.arange(BLK, dtype=jnp.int32)
        k_pos = row_start - WIN + jnp.arange(window_span, dtype=jnp.int32)
        near_ok = (k_pos[None, :] <= q_pos[:, None]) & (q_pos[:, None] - k_pos[None, :] < WIN) & (k_pos[None, :] >= 0)
        far_ok = jnp.broadcast_to(jnp.repeat(is_live, BLK)[None, :], (BLK, LINKS * BLK))
        is_valid = jnp.concatenate([near_ok, far_ok], axis=1)
        query_grad, key_value_gradient = block_grads(query_row_block, gradient_row_block, key_tile[:, :half_width], key_tile[:, half_width:], is_valid)
        current = lax.dynamic_slice_in_dim(acc, row_start, window_span, 0)
        acc = lax.dynamic_update_slice_in_dim(acc, current + key_value_gradient[:window_span], row_start, 0)
        for slot in range(LINKS):
            target = (WIN + header_ids[slot] * BLK).astype(jnp.int32)
            extra = key_value_gradient[window_span + slot * BLK: window_span + (slot + 1) * BLK] * is_live[slot].astype(jnp.float32)
            current = lax.dynamic_slice_in_dim(acc, target, BLK, 0)
            acc = lax.dynamic_update_slice_in_dim(acc, current + extra, target, 0)
        return acc, query_grad.astype(jnp.bfloat16)

    start_acc = jnp.zeros((seq_len + WIN, kv_width), jnp.float32)
    acc, dq_blocks = lax.scan(one_block, start_acc, jnp.arange(block_total, dtype=jnp.int32))
    query_out = dq_blocks.reshape(seq_len, QUERY_HEADS * HEAD_SIZE)
    full_grad = acc[WIN:]
    return query_out, full_grad[:, :half_width], full_grad[:, half_width:]
```

```python
import functools

import jax
import jax.numpy as jnp
from jax import lax
from jax.experimental import pallas as pl
from jax.experimental.pallas import tpu as pltpu
from jax.sharding import PartitionSpec as P

QUERY_HEADS = 28
KEY_VALUE_HEADS = 4
HEAD_SIZE = 128
BLK = 128
WIN = 256
LINKS = 4
RATIO = QUERY_HEADS // KEY_VALUE_HEADS
LANES = RATIO * BLK
SPAN = WIN + BLK
FACTOR = float(HEAD_SIZE) ** (-0.5)
LOG2E = 1.4426950408889634
DEAD = -1e30
CHUNKS = tuple((at, min(at + 2, RATIO)) for at in range(0, RATIO, 2))

NT = (((1,), (1,)), ((), ()))
NN = (((1,), (0,)), ((), ()))
TN = (((0,), (0,)), ((), ()))


def dot(a, b, dims):
    return lax.dot_general(a, b, dims, preferred_element_type=jnp.float32)


def stacked(ref, lo, hi):
    return jnp.concatenate(
        [ref[:, r * HEAD_SIZE : (r + 1) * HEAD_SIZE] for r in range(lo, hi)], axis=0
    )


def head_kernel(
    heads_ref, links_ref, block_ref, q_ref, g_ref, kw_ref, vw_ref, kh_ref, vh_ref, *rest
):
    (dq_ref, dkw_ref, dvw_ref, dkh_ref, dvh_ref) = rest[-13:-8]
    (w_ref, da_ref, m_ref, l_ref, u_ref, dqt_ref, dkh_acc, dvh_acc) = rest[-8:]
    b = pl.program_id(1)
    last = pl.num_programs(1) - 1
    start = pl.multiple_of(b * BLK, BLK)
    block_id = block_ref[0] + b

    @pl.when(b == 0)
    def _():
        dkw_ref[...] = jnp.zeros_like(dkw_ref)
        dvw_ref[...] = jnp.zeros_like(dvw_ref)
        dkh_acc[...] = jnp.zeros_like(dkh_acc)
        dvh_acc[...] = jnp.zeros_like(dvh_acc)

    first_bias = jnp.where(block_id >= 2, 0.0, DEAD).astype(jnp.float32)
    mid_bias = jnp.where(block_id >= 1, 0.0, DEAD).astype(jnp.float32)

    def triangle(width):
        key_row = lax.broadcasted_iota(jnp.int32, (BLK, width), 0)
        query_row = lax.broadcasted_iota(jnp.int32, (BLK, width), 1) % BLK
        return key_row <= query_row

    k_win = kw_ref[pl.ds(start, SPAN), :]
    v_win = vw_ref[pl.ds(start, SPAN), :]
    for lo, hi in CHUNKS:
        lanes = slice(lo * BLK, hi * BLK)
        own = triangle((hi - lo) * BLK)
        s = dot(k_win, stacked(q_ref, lo, hi), NT)
        s_edge = jnp.where(own, s[2 * BLK :], s[:BLK] + first_bias) * (FACTOR * LOG2E)
        s_mid = s[BLK : 2 * BLK] * (FACTOR * LOG2E)
        m = jnp.maximum(
            jnp.max(s_edge, axis=0, keepdims=True),
            jnp.max(s_mid, axis=0, keepdims=True) + mid_bias,
        )
        w_edge = jnp.exp2(s_edge - m)
        w_mid = jnp.exp2(s_mid - (m - mid_bias))
        da = dot(v_win, stacked(g_ref, lo, hi), NT)
        da_edge = jnp.where(own, da[2 * BLK :], da[:BLK])
        da_mid = da[BLK : 2 * BLK]
        m_ref[0:1, lanes] = m
        l_ref[:, lanes] = jnp.sum(w_edge + w_mid, axis=0, keepdims=True)
        u_ref[:, lanes] = jnp.sum(w_edge * da_edge + w_mid * da_mid, axis=0, keepdims=True)
        w_ref[0:BLK, lanes] = w_edge
        w_ref[BLK : 2 * BLK, lanes] = w_mid
        da_ref[0:BLK, lanes] = da_edge
        da_ref[BLK : 2 * BLK, lanes] = da_mid
    m_ref[LINKS + 1 : LINKS + 2, :] = m_ref[0:1, :]

    for e in range(LINKS):
        entry = links_ref[b, e]

        @pl.when(entry >= 0)
        def _(e=e, entry=entry):
            k_head = kh_ref[entry]
            v_head = vh_ref[entry]
            rows = slice(WIN + e * BLK, WIN + (e + 1) * BLK)
            for lo, hi in CHUNKS:
                lanes = slice(lo * BLK, hi * BLK)
                s = dot(k_head, stacked(q_ref, lo, hi), NT) * (FACTOR * LOG2E)
                m = jnp.max(s, axis=0, keepdims=True)
                w = jnp.exp2(s - m)
                da = dot(v_head, stacked(g_ref, lo, hi), NT)
                l = jnp.sum(w, axis=0, keepdims=True)
                u = jnp.sum(w * da, axis=0, keepdims=True)
                m_old = m_ref[LINKS + 1 : LINKS + 2, lanes]
                m_new = jnp.maximum(m_old, m)
                old = jnp.exp2(m_old - m_new)
                new = jnp.exp2(m - m_new)
                m_ref[e + 1 : e + 2, lanes] = m
                m_ref[LINKS + 1 : LINKS + 2, lanes] = m_new
                l_ref[:, lanes] = l_ref[:, lanes] * old + l * new
                u_ref[:, lanes] = u_ref[:, lanes] * old + u * new
                w_ref[rows, lanes] = w
                da_ref[rows, lanes] = da

    m_all = m_ref[LINKS + 1 : LINKS + 2, :]
    inv = 1.0 / l_ref[...]
    delta = u_ref[...] * inv
    u_ref[...] = delta
    l_ref[...] = inv

    dk = None
    dv = None
    alpha_all = jnp.exp2(m_ref[0:1, :] - m_all) * inv
    for lo, hi in CHUNKS:
        lanes = slice(lo * BLK, hi * BLK)
        own = triangle((hi - lo) * BLK)
        alpha = alpha_all[:, lanes]
        dlt = delta[:, lanes]
        zero = jnp.zeros((BLK, (hi - lo) * BLK), jnp.float32)
        p_edge = w_ref[0:BLK, lanes] * alpha
        p_mid = w_ref[BLK : 2 * BLK, lanes] * alpha
        ds_edge = p_edge * (da_ref[0:BLK, lanes] - dlt)
        ds_mid = p_mid * (da_ref[BLK : 2 * BLK, lanes] - dlt)
        p = jnp.concatenate(
            [jnp.where(own, zero, p_edge), p_mid, jnp.where(own, p_edge, zero)], axis=0
        ).astype(jnp.bfloat16)
        ds = jnp.concatenate(
            [jnp.where(own, zero, ds_edge), ds_mid, jnp.where(own, ds_edge, zero)], axis=0
        ).astype(jnp.bfloat16)
        dv_part = dot(p, stacked(g_ref, lo, hi), NN)
        dk_part = dot(ds, stacked(q_ref, lo, hi), NN)
        dv = dv_part if dv is None else dv + dv_part
        dk = dk_part if dk is None else dk + dk_part
        dqt_ref[:, lanes] = dot(k_win, ds, TN)
    dkw_ref[pl.ds(start, SPAN), :] += dk * FACTOR
    dvw_ref[pl.ds(start, SPAN), :] += dv

    for e in range(LINKS):
        entry = links_ref[b, e]

        @pl.when(entry >= 0)
        def _(e=e, entry=entry):
            k_head = kh_ref[entry]
            rows = slice(WIN + e * BLK, WIN + (e + 1) * BLK)
            alpha_all = jnp.exp2(
                m_ref[e + 1 : e + 2, :] - m_ref[LINKS + 1 : LINKS + 2, :]
            ) * l_ref[...]
            dk = None
            dv = None
            for lo, hi in CHUNKS:
                lanes = slice(lo * BLK, hi * BLK)
                p = w_ref[rows, lanes] * alpha_all[:, lanes]
                ds = (p * (da_ref[rows, lanes] - u_ref[:, lanes])).astype(jnp.bfloat16)
                p = p.astype(jnp.bfloat16)
                dv_part = dot(p, stacked(g_ref, lo, hi), NN)
                dk_part = dot(ds, stacked(q_ref, lo, hi), NN)
                dv = dv_part if dv is None else dv + dv_part
                dk = dk_part if dk is None else dk + dk_part
                dqt_ref[:, lanes] += dot(k_head, ds, TN)
            dkh_acc[entry] += dk
            dvh_acc[entry] += dv

    for r in range(RATIO):
        lanes = slice(r * BLK, (r + 1) * BLK)
        dq_ref[:, lanes] = (dqt_ref[:, lanes].T * FACTOR).astype(jnp.bfloat16)

    @pl.when(b == last)
    def _():
        dkh_ref[0] = (dkh_acc[...] * FACTOR).astype(dkh_ref.dtype)
        dvh_ref[0] = dvh_acc[...].astype(dvh_ref.dtype)


def head_grads(heads, links, first_block, queries, out_grad, k_ext, v_ext, k_head, v_head, carried):
    count, headers = k_head.shape[:2]
    rows = queries.shape[0]
    blocks = rows // BLK
    ext = k_ext.shape[0]
    wide = pl.BlockSpec((BLK, LANES), lambda i, b, h, *_: (b, h[i]))
    narrow = pl.BlockSpec((ext, HEAD_SIZE), lambda i, b, h, *_: (0, h[i]))
    table = pl.BlockSpec((None, headers, BLK, HEAD_SIZE), lambda i, b, *_: (i, 0, 0, 0))
    table_out = pl.BlockSpec((1, headers, BLK, HEAD_SIZE), lambda i, b, *_: (i, 0, 0, 0))
    anywhere = pl.BlockSpec(memory_space=pl.ANY)
    carried = tuple(carried)
    places = LINKS * BLK + WIN
    return pl.pallas_call(
        head_kernel,
        grid_spec=pltpu.PrefetchScalarGridSpec(
            num_scalar_prefetch=3,
            grid=(count, blocks),
            in_specs=[wide, wide, narrow, narrow, table, table] + [anywhere] * len(carried),
            out_specs=[wide, narrow, narrow, table_out, table_out],
            scratch_shapes=[
                pltpu.VMEM((places, LANES), jnp.float32),
                pltpu.VMEM((places, LANES), jnp.float32),
                pltpu.VMEM((8, LANES), jnp.float32),
                pltpu.VMEM((1, LANES), jnp.float32),
                pltpu.VMEM((1, LANES), jnp.float32),
                pltpu.VMEM((HEAD_SIZE, LANES), jnp.float32),
                pltpu.VMEM((headers, BLK, HEAD_SIZE), jnp.float32),
                pltpu.VMEM((headers, BLK, HEAD_SIZE), jnp.float32),
            ],
        ),
        out_shape=[
            jax.ShapeDtypeStruct(queries.shape, jnp.bfloat16),
            jax.ShapeDtypeStruct(k_ext.shape, jnp.float32),
            jax.ShapeDtypeStruct(v_ext.shape, jnp.float32),
            jax.ShapeDtypeStruct((count, headers, BLK, HEAD_SIZE), jnp.bfloat16),
            jax.ShapeDtypeStruct((count, headers, BLK, HEAD_SIZE), jnp.bfloat16),
        ],
        input_output_aliases={9 + i: i for i in range(len(carried))},
        compiler_params=pltpu.CompilerParams(
            dimension_semantics=("arbitrary", "arbitrary"), vmem_limit_bytes=48 * 1024 * 1024
        ),
        cost_estimate=pl.CostEstimate(
            flops=count * blocks * 5 * 2 * BLK * LANES * HEAD_SIZE * 6,
            bytes_accessed=count * rows * LANES * 6,
            transcendentals=0,
        ),
    )(heads, links, first_block, queries, out_grad, k_ext, v_ext, k_head, v_head, *carried)


def xor_permute(x, mask):
    peers = lax.axis_size("ctx")
    return lax.ppermute(x, "ctx", [(i, i ^ mask) for i in range(peers)])


def shifted(x, by):
    peers = lax.axis_size("ctx")
    pairs = [(i, i + by) for i in range(peers) if 0 <= i + by < peers]
    return lax.ppermute(x, "ctx", pairs)


def pick(table, index):
    return lax.dynamic_index_in_dim(table, index, 0, keepdims=False)


def body(queries, keys, values, out_grad, links, header_blocks):
    rows = queries.shape[0]
    blocks = rows // BLK
    headers = header_blocks.shape[0]
    peers = lax.axis_size("ctx")
    me = lax.axis_index("ctx")
    low = me & 3
    high = me >> 2
    core = me & 1
    side = low >> 1
    owners = header_blocks // blocks
    mine = owners == me
    offset = jnp.sum(jnp.where(mine, header_blocks % blocks, 0))

    k_ext = jnp.concatenate([shifted(keys[rows - WIN :], 1), keys], axis=0)
    v_ext = jnp.concatenate([shifted(values[rows - WIN :], 1), values], axis=0)

    def by_head(x):
        x = lax.dynamic_slice_in_dim(x, offset * BLK, BLK, 0)
        return x.reshape(BLK, KEY_VALUE_HEADS, HEAD_SIZE).transpose(1, 0, 2)

    slot = jnp.concatenate([by_head(keys), by_head(values)], axis=2)
    slot = slot.reshape(2, 2, BLK, 2 * HEAD_SIZE)
    keep = lax.dynamic_index_in_dim(slot, core, 1, keepdims=False)
    give = lax.dynamic_index_in_dim(slot, 1 - core, 1, keepdims=False)
    got = xor_permute(give, 1)
    pair = jnp.where(core == 0, jnp.stack([keep, got]), jnp.stack([got, keep]))
    keep = lax.dynamic_index_in_dim(pair, side, 1, keepdims=False)
    give = lax.dynamic_index_in_dim(pair, 1 - side, 1, keepdims=False)
    got = xor_permute(give, 2)
    plane = jnp.where(side == 0, jnp.concatenate([keep, got]), jnp.concatenate([got, keep]))
    mine_table = plane[owners & 3]
    step = 0
    while (4 << step) < peers:
        got = xor_permute(mine_table, 4 << step)
        from_peer = (owners >> (2 + step)) == ((high >> step) ^ 1)
        mine_table = jnp.where(from_peer[:, None, None], got, mine_table)
        step += 1
    other_side = xor_permute(mine_table, 2)
    two = jnp.stack([mine_table, other_side])
    other_core = xor_permute(two, 1)
    tables = jnp.concatenate([two, other_core])
    heads = jnp.stack([low, low ^ 2, low ^ 1, low ^ 3]).astype(jnp.int32)

    first_block = (me * blocks).astype(jnp.int32).reshape(1)
    query_grad, dk_ext, dv_ext, dk_head, dv_head = head_grads(
        heads, links, first_block, queries, out_grad, k_ext, v_ext,
        tables[..., :HEAD_SIZE], tables[..., HEAD_SIZE:], (),
    )

    back = jnp.concatenate([dk_ext[:WIN], dv_ext[:WIN]], axis=1).astype(jnp.bfloat16)
    back = shifted(back, -1).astype(jnp.float32)

    parts = jnp.concatenate([dk_head, dv_head], axis=3)
    total = parts[0].astype(jnp.float32)
    for at, mask in ((1, 2), (2, 1), (3, 3)):
        total = total + xor_permute(parts[at], mask).astype(jnp.float32)
    while step > 0:
        step -= 1
        low_total = total.astype(jnp.bfloat16)
        total = total + xor_permute(low_total, 4 << step).astype(jnp.float32)
    wanted = owners[None, :] == (high * 4 + jnp.arange(4, dtype=jnp.int32))[:, None]
    owned = jnp.sum(
        jnp.where(wanted[:, :, None, None], total[None], 0.0), axis=1
    ).astype(jnp.bfloat16)
    owned = owned.reshape(2, 2, BLK, 2 * HEAD_SIZE)
    keep = pick(owned, side)
    got = xor_permute(pick(owned, 1 - side), 2)
    pair = jnp.where(side == 0, jnp.stack([keep, got]), jnp.stack([got, keep]))
    keep = lax.dynamic_index_in_dim(pair, core, 1, keepdims=False)
    give = lax.dynamic_index_in_dim(pair, 1 - core, 1, keepdims=False)
    got = xor_permute(give, 1)
    full = jnp.where(core == 0, jnp.stack([keep, got], axis=1), jnp.stack([got, keep], axis=1))
    full = full.reshape(KEY_VALUE_HEADS, BLK, 2 * HEAD_SIZE).astype(jnp.float32)

    def finish(grad, returned, own):
        grad = grad[WIN:]
        grad = grad.at[rows - WIN :].add(returned)
        own = own.transpose(1, 0, 2).reshape(BLK, KEY_VALUE_HEADS * HEAD_SIZE)
        spread = (jnp.arange(blocks, dtype=jnp.int32) == offset) & jnp.any(mine)
        own = jnp.where(spread[:, None, None], own[None], 0.0)
        return grad + own.reshape(rows, KEY_VALUE_HEADS * HEAD_SIZE)

    half = KEY_VALUE_HEADS * HEAD_SIZE
    return (
        query_grad,
        finish(dk_ext, back[:, :half], full[..., :HEAD_SIZE]),
        finish(dv_ext, back[:, half:], full[..., HEAD_SIZE:]),
    )


def solution(mesh):
    rows = P(("groups", "ctx"), None)
    return jax.shard_map(
        body,
        mesh=mesh,
        in_specs=(rows, rows, rows, rows, rows, P("groups")),
        out_specs=(rows, rows, rows),
        check_vma=False,
    )
```

```python
import functools

import jax
import jax.numpy as jnp
from jax import lax
from jax.experimental import pallas as pl
from jax.experimental.pallas import tpu as pltpu
from jax.sharding import PartitionSpec as P

QUERY_HEADS = 28
KEY_VALUE_HEADS = 4
HEAD_SIZE = 128
BLK = 128
WIN = 256
LINKS = 4
RATIO = QUERY_HEADS // KEY_VALUE_HEADS
LANES = RATIO * BLK
SPAN = WIN + BLK
FACTOR = float(HEAD_SIZE) ** (-0.5)
LOG2E = 1.4426950408889634
DEAD = -1e30
SCALE = FACTOR * LOG2E
TILE = 16
CHUNKS = tuple((at, min(at + 2, RATIO)) for at in range(0, RATIO, 2))

NT = (((1,), (1,)), ((), ()))
NN = (((1,), (0,)), ((), ()))


def dot(a, b, dims):
    return lax.dot_general(a, b, dims, preferred_element_type=jnp.float32)


def stacked(ref, lo, hi):
    return jnp.concatenate(
        [ref[:, r * HEAD_SIZE : (r + 1) * HEAD_SIZE] for r in range(lo, hi)], axis=0
    )


def extend(ext_ref, halo_ref, own_ref):
    ext_ref[0:WIN, :] = halo_ref[...]
    ext_ref[WIN:, :] = own_ref[...]


def dead_biases(block_id):
    first = jnp.where(block_id >= 2, 0.0, DEAD).astype(jnp.float32)
    mid = jnp.where(block_id >= 1, 0.0, DEAD).astype(jnp.float32)
    return first, mid


def queries_ahead(width):
    key_row = lax.broadcasted_iota(jnp.int32, (TILE, width), 0)
    query_row = lax.broadcasted_iota(jnp.int32, (TILE, width), 1) % BLK
    return query_row - key_row


def pair_scores(at, k, v, q_ref, g_ref, s_ref, da_ref):
    lo, hi = CHUNKS[at]
    width = (hi - lo) * BLK
    places = k.shape[0]
    s_ref[at % 2, 0:places, 0:width] = dot(k, stacked(q_ref, lo, hi), NT)
    da_ref[at % 2, 0:places, 0:width] = dot(v, stacked(g_ref, lo, hi), NT)


def window_stats_kernel(
    heads_ref, block_ref, q_ref, g_ref, k_halo, v_halo, k_own, v_own, stat_ref,
    k_ext, v_ext, s_ref, da_ref,
):
    b = pl.program_id(1)
    start = pl.multiple_of(b * BLK, BLK)

    @pl.when(b == 0)
    def _():
        extend(k_ext, k_halo, k_own)
        extend(v_ext, v_halo, v_own)

    first_bias, mid_bias = dead_biases(block_ref[0] + b)
    k = k_ext[pl.ds(start, SPAN), :]
    v = v_ext[pl.ds(start, SPAN), :]

    def stats(at):
        lo, hi = CHUNKS[at]
        width = (hi - lo) * BLK
        lanes = slice(lo * BLK, hi * BLK)
        s_at, da_at = s_ref.at[at % 2], da_ref.at[at % 2]
        ahead = queries_ahead(width)

        def tile(ref, row):
            return ref[row : row + TILE, 0:width]

        m = None
        m_mid = None
        for t in range(0, BLK, TILE):
            x = jnp.where(ahead >= t, tile(s_at, 2 * BLK + t), tile(s_at, t) + first_bias)
            s_at[2 * BLK + t : 2 * BLK + t + TILE, 0:width] = x
            m = x if m is None else jnp.maximum(m, x)
            x = tile(s_at, BLK + t)
            m_mid = x if m_mid is None else jnp.maximum(m_mid, x)
        m = jnp.maximum(m, m_mid + mid_bias)
        m = jnp.max(m, axis=0, keepdims=True) * SCALE
        m_mid = m - mid_bias
        l = jnp.zeros((TILE, width), jnp.float32)
        u = jnp.zeros((TILE, width), jnp.float32)
        for t in range(0, BLK, TILE):
            w = jnp.exp2(tile(s_at, 2 * BLK + t) * SCALE - m)
            da = jnp.where(ahead >= t, tile(da_at, 2 * BLK + t), tile(da_at, t))
            l = l + w
            u = u + w * da
            w = jnp.exp2(tile(s_at, BLK + t) * SCALE - m_mid)
            l = l + w
            u = u + w * tile(da_at, BLK + t)
        stat_ref[0:1, lanes] = m
        stat_ref[1:2, lanes] = jnp.sum(l, axis=0, keepdims=True)
        stat_ref[2:3, lanes] = jnp.sum(u, axis=0, keepdims=True)

    pair_scores(0, k, v, q_ref, g_ref, s_ref, da_ref)
    for at in range(len(CHUNKS)):
        if at + 1 < len(CHUNKS):
            pair_scores(at + 1, k, v, q_ref, g_ref, s_ref, da_ref)
        stats(at)


def header_kernel(
    heads_ref, links_ref, q_ref, g_ref, kh_ref, vh_ref, stat_ref,
    fin_ref, dqt_ref, dkh_ref, s_ref, da_ref, p_ref, ds_ref, dkh_acc, dvh_acc, ids_ref,
):
    b = pl.program_id(1)
    last = pl.num_programs(1) - 1

    @pl.when(b == 0)
    def _():
        dkh_acc[...] = jnp.zeros_like(dkh_acc)
        dvh_acc[...] = jnp.zeros_like(dvh_acc)

    live = jnp.int32(0)
    for e in range(LINKS):
        entry = links_ref[b, e]

        @pl.when(entry >= 0)
        def _(entry=entry, live=live):
            ids_ref[live] = entry

        live = live + jnp.where(entry >= 0, 1, 0)

    @pl.when(live == 0)
    def _():
        l = stat_ref[1:2, :]
        fin_ref[0:1, :] = stat_ref[0:1, :] + jnp.log2(l)
        fin_ref[1:2, :] = stat_ref[2:3, :] / l
        dqt_ref[...] = jnp.zeros_like(dqt_ref)

    def block(count):
        ids = [ids_ref[j] for j in range(count)]
        k = jnp.concatenate([kh_ref[i] for i in ids], axis=0)
        v = jnp.concatenate([vh_ref[i] for i in ids], axis=0)
        places = count * BLK

        def weights(at):
            lo, hi = CHUNKS[at]
            width = (hi - lo) * BLK
            lanes = slice(lo * BLK, hi * BLK)
            s_at, da_at = s_ref.at[at % 2], da_ref.at[at % 2]

            def tile(ref, row):
                return ref[row : row + TILE, 0:width]

            m = tile(s_at, 0)
            for row in range(TILE, places, TILE):
                m = jnp.maximum(m, tile(s_at, row))
            before = stat_ref[0:1, lanes]
            m = jnp.maximum(before, jnp.max(m, axis=0, keepdims=True) * SCALE)
            l = jnp.zeros((TILE, width), jnp.float32)
            u = jnp.zeros((TILE, width), jnp.float32)
            for row in range(0, places, TILE):
                w = jnp.exp2(tile(s_at, row) * SCALE - m)
                s_at[row : row + TILE, 0:width] = w
                l = l + w
                u = u + w * tile(da_at, row)
            keep = jnp.exp2(before - m)
            l = jnp.sum(l, axis=0, keepdims=True) + keep * stat_ref[1:2, lanes]
            u = jnp.sum(u, axis=0, keepdims=True) + keep * stat_ref[2:3, lanes]
            inv = 1.0 / l
            delta = u * inv
            fin_ref[0:1, lanes] = m + jnp.log2(l)
            fin_ref[1:2, lanes] = delta
            for row in range(0, places, TILE):
                p = tile(s_at, row) * inv
                ds = p * (tile(da_at, row) - delta)
                p_ref[row : row + TILE, lanes] = p.astype(jnp.bfloat16)
                ds_ref[row : row + TILE, lanes] = ds.astype(jnp.bfloat16)

        pair_scores(0, k, v, q_ref, g_ref, s_ref, da_ref)
        for at in range(len(CHUNKS)):
            if at + 1 < len(CHUNKS):
                pair_scores(at + 1, k, v, q_ref, g_ref, s_ref, da_ref)
            weights(at)
        dqt_ref[...] = dot(k.T, ds_ref[0:places, :], NN)
        dk = dot(ds_ref[0:places, :], stacked(q_ref, 0, RATIO), NN)
        dv = dot(p_ref[0:places, :], stacked(g_ref, 0, RATIO), NN)
        for j, i in enumerate(ids):
            rows = slice(j * BLK, (j + 1) * BLK)
            dkh_acc[i] += dk[rows]
            dvh_acc[i] += dv[rows]

    for count in range(1, LINKS + 1):
        pl.when(live == count)(functools.partial(block, count))

    @pl.when(b == last)
    def _():
        dkh_ref[:, :, 0:HEAD_SIZE] = (dkh_acc[...] * FACTOR).astype(dkh_ref.dtype)
        dkh_ref[:, :, HEAD_SIZE:] = dvh_acc[...].astype(dkh_ref.dtype)


def window_grads_kernel(
    heads_ref, block_ref, q_ref, g_ref, k_halo, v_halo, k_own, v_own, fin_ref, dqt_ref, *rest
):
    (dq_ref, dk_ref, dv_ref, back_ref) = rest[-12:-8]
    (k_ext, v_ext, s_ref, da_ref, p_ref, ds_ref, dk_acc, dv_acc) = rest[-8:]
    b = pl.program_id(1)
    last = pl.num_programs(1) - 1
    start = pl.multiple_of(b * BLK, BLK)

    @pl.when(b == 0)
    def _():
        extend(k_ext, k_halo, k_own)
        extend(v_ext, v_halo, v_own)
        dk_acc[...] = jnp.zeros_like(dk_acc)
        dv_acc[...] = jnp.zeros_like(dv_acc)

    first_bias, mid_bias = dead_biases(block_ref[0] + b)
    k = k_ext[pl.ds(start, SPAN), :]
    v = v_ext[pl.ds(start, SPAN), :]

    def weights(at):
        lo, hi = CHUNKS[at]
        width = (hi - lo) * BLK
        lanes = slice(lo * BLK, hi * BLK)
        s_at, da_at = s_ref.at[at % 2], da_ref.at[at % 2]
        ahead = queries_ahead(width)
        top = fin_ref[0:1, lanes]
        delta = fin_ref[1:2, lanes]
        top_mid = top - mid_bias

        def tile(ref, row):
            return ref[row : row + TILE, 0:width]

        for t in range(0, BLK, TILE):
            own = ahead >= t
            s = jnp.where(own, tile(s_at, 2 * BLK + t), tile(s_at, t) + first_bias)
            da = jnp.where(own, tile(da_at, 2 * BLK + t), tile(da_at, t))
            p = jnp.exp2(s * SCALE - top)
            ds = p * (da - delta)
            for ref, x in ((p_ref, p), (ds_ref, ds)):
                ref[2 * BLK + t : 2 * BLK + t + TILE, lanes] = jnp.where(own, x, 0.0).astype(jnp.bfloat16)
                ref[t : t + TILE, lanes] = jnp.where(own, 0.0, x).astype(jnp.bfloat16)
            p = jnp.exp2(tile(s_at, BLK + t) * SCALE - top_mid)
            ds = p * (tile(da_at, BLK + t) - delta)
            p_ref[BLK + t : BLK + t + TILE, lanes] = p.astype(jnp.bfloat16)
            ds_ref[BLK + t : BLK + t + TILE, lanes] = ds.astype(jnp.bfloat16)

    pair_scores(0, k, v, q_ref, g_ref, s_ref, da_ref)
    for at in range(len(CHUNKS)):
        if at + 1 < len(CHUNKS):
            pair_scores(at + 1, k, v, q_ref, g_ref, s_ref, da_ref)
        weights(at)
    dqt = (dot(k.T, ds_ref[...], NN) + dqt_ref[...]) * FACTOR
    for r in range(RATIO):
        lanes = slice(r * BLK, (r + 1) * BLK)
        dq_ref[:, lanes] = dqt[:, lanes].astype(jnp.bfloat16).T
    dk_acc[pl.ds(start, SPAN), :] += dot(ds_ref[...], stacked(q_ref, 0, RATIO), NN)
    dv_acc[pl.ds(start, SPAN), :] += dot(p_ref[...], stacked(g_ref, 0, RATIO), NN)

    @pl.when(b == last)
    def _():
        dk_ref[...] = dk_acc[WIN:, :] * FACTOR
        dv_ref[...] = dv_acc[WIN:, :]
        back_ref[0] = (dk_acc[0:WIN, :] * FACTOR).astype(back_ref.dtype)
        back_ref[1] = dv_acc[0:WIN, :].astype(back_ref.dtype)


PARAMS = pltpu.CompilerParams(
    dimension_semantics=("arbitrary", "arbitrary"), vmem_limit_bytes=40 * 1024 * 1024
)


def estimate(count, blocks, places, matmuls):
    flops = 2 * count * blocks * matmuls * places * LANES * HEAD_SIZE
    return pl.CostEstimate(
        flops=flops, bytes_accessed=count * blocks * BLK * LANES * 6, transcendentals=0
    )


def wide_spec():
    return pl.BlockSpec((BLK, LANES), lambda i, b, h, *_: (b, h[i]))


def column_spec(rows, shift=0):
    return pl.BlockSpec((rows, HEAD_SIZE), lambda i, b, h, *_: (0, h[i] + shift))


def row_spec(rows):
    return pl.BlockSpec((None, None, rows, LANES), lambda i, b, *_: (i, b, 0, 0))


def pair_scratch(places):
    return [pltpu.VMEM((2, places, 2 * BLK), jnp.float32)] * 2


def window_operands(queries, out_grad, halo, keys, values):
    rows = keys.shape[0]
    specs = [
        wide_spec(), wide_spec(), column_spec(WIN), column_spec(WIN, KEY_VALUE_HEADS),
        column_spec(rows), column_spec(rows),
    ]
    return specs, (queries, out_grad, halo, halo, keys, values)


def window_stats(heads, first_block, queries, out_grad, halo, keys, values):
    count = heads.shape[0]
    rows = queries.shape[0]
    blocks = rows // BLK
    specs, operands = window_operands(queries, out_grad, halo, keys, values)
    return pl.pallas_call(
        window_stats_kernel,
        grid_spec=pltpu.PrefetchScalarGridSpec(
            num_scalar_prefetch=2,
            grid=(count, blocks),
            in_specs=specs,
            out_specs=row_spec(8),
            scratch_shapes=[pltpu.VMEM((WIN + rows, HEAD_SIZE), jnp.bfloat16)] * 2
            + pair_scratch(SPAN),
        ),
        out_shape=jax.ShapeDtypeStruct((count, blocks, 8, LANES), jnp.float32),
        compiler_params=PARAMS,
        cost_estimate=estimate(count, blocks, SPAN, 5),
    )(heads, first_block, *operands)


def header_grads(heads, links, queries, out_grad, k_head, v_head, stats):
    count, headers = k_head.shape[:2]
    blocks = queries.shape[0] // BLK
    table = pl.BlockSpec((None, headers, BLK, HEAD_SIZE), lambda i, b, *_: (i, 0, 0, 0))
    both = pl.BlockSpec((None, headers, BLK, 2 * HEAD_SIZE), lambda i, b, *_: (i, 0, 0, 0))
    return pl.pallas_call(
        header_kernel,
        grid_spec=pltpu.PrefetchScalarGridSpec(
            num_scalar_prefetch=2,
            grid=(count, blocks),
            in_specs=[wide_spec(), wide_spec(), table, table, row_spec(8)],
            out_specs=[row_spec(8), row_spec(HEAD_SIZE), both],
            scratch_shapes=pair_scratch(LINKS * BLK)
            + [pltpu.VMEM((LINKS * BLK, LANES), jnp.bfloat16)] * 2
            + [pltpu.VMEM((headers, BLK, HEAD_SIZE), jnp.float32)] * 2
            + [pltpu.SMEM((LINKS,), jnp.int32)],
        ),
        out_shape=[
            jax.ShapeDtypeStruct((count, blocks, 8, LANES), jnp.float32),
            jax.ShapeDtypeStruct((count, blocks, HEAD_SIZE, LANES), jnp.float32),
            jax.ShapeDtypeStruct((count, headers, BLK, 2 * HEAD_SIZE), jnp.bfloat16),
        ],
        compiler_params=PARAMS,
        cost_estimate=estimate(count, blocks, 3 * BLK, 7),
    )(heads, links, queries, out_grad, k_head, v_head, stats)


def window_grads(heads, first_block, queries, out_grad, halo, keys, values, fin, dqt, carried):
    count = heads.shape[0]
    rows = queries.shape[0]
    blocks = rows // BLK
    specs, operands = window_operands(queries, out_grad, halo, keys, values)
    carried = tuple(carried)
    first = 2 + len(specs) + 2
    return pl.pallas_call(
        window_grads_kernel,
        grid_spec=pltpu.PrefetchScalarGridSpec(
            num_scalar_prefetch=2,
            grid=(count, blocks),
            in_specs=specs
            + [row_spec(8), row_spec(HEAD_SIZE)]
            + [pl.BlockSpec(memory_space=pl.ANY)] * len(carried),
            out_specs=[
                wide_spec(), column_spec(rows), column_spec(rows),
                pl.BlockSpec((2, WIN, HEAD_SIZE), lambda i, b, h, *_: (0, 0, h[i])),
            ],
            scratch_shapes=[pltpu.VMEM((WIN + rows, HEAD_SIZE), jnp.bfloat16)] * 2
            + pair_scratch(SPAN)
            + [pltpu.VMEM((SPAN, LANES), jnp.bfloat16)] * 2
            + [pltpu.VMEM((WIN + rows, HEAD_SIZE), jnp.float32)] * 2,
        ),
        out_shape=[
            jax.ShapeDtypeStruct(queries.shape, jnp.bfloat16),
            jax.ShapeDtypeStruct(keys.shape, jnp.float32),
            jax.ShapeDtypeStruct(values.shape, jnp.float32),
            jax.ShapeDtypeStruct((2, WIN, keys.shape[1]), jnp.bfloat16),
        ],
        input_output_aliases={first + i: i for i in range(len(carried))},
        compiler_params=PARAMS,
        cost_estimate=estimate(count, blocks, SPAN, 8),
    )(heads, first_block, *operands, fin, dqt, *carried)


def xor_permute(x, mask):
    peers = lax.axis_size("ctx")
    return lax.ppermute(x, "ctx", [(i, i ^ mask) for i in range(peers)])


def shifted(x, by):
    peers = lax.axis_size("ctx")
    pairs = [(i, i + by) for i in range(peers) if 0 <= i + by < peers]
    return lax.ppermute(x, "ctx", pairs)


def pick(table, index):
    return lax.dynamic_index_in_dim(table, index, 0, keepdims=False)


def body(queries, keys, values, out_grad, links, header_blocks):
    rows = queries.shape[0]
    blocks = rows // BLK
    headers = header_blocks.shape[0]
    peers = lax.axis_size("ctx")
    me = lax.axis_index("ctx")
    low = me & 3
    high = me >> 2
    core = me & 1
    side = low >> 1
    owners = header_blocks // blocks
    mine = owners == me
    offset = jnp.sum(jnp.where(mine, header_blocks % blocks, 0))

    halo = shifted(jnp.concatenate([keys[rows - WIN :], values[rows - WIN :]], axis=1), 1)

    def by_head(x):
        x = lax.dynamic_slice_in_dim(x, offset * BLK, BLK, 0)
        return x.reshape(BLK, KEY_VALUE_HEADS, HEAD_SIZE).transpose(1, 0, 2)

    slot = jnp.concatenate([by_head(keys), by_head(values)], axis=2)
    slot = slot.reshape(2, 2, BLK, 2 * HEAD_SIZE)
    keep = lax.dynamic_index_in_dim(slot, core, 1, keepdims=False)
    give = lax.dynamic_index_in_dim(slot, 1 - core, 1, keepdims=False)
    got = xor_permute(give, 1)
    pair = jnp.where(core == 0, jnp.stack([keep, got]), jnp.stack([got, keep]))
    keep = lax.dynamic_index_in_dim(pair, side, 1, keepdims=False)
    give = lax.dynamic_index_in_dim(pair, 1 - side, 1, keepdims=False)
    got = xor_permute(give, 2)
    plane = jnp.where(side == 0, jnp.concatenate([keep, got]), jnp.concatenate([got, keep]))
    mine_table = plane[owners & 3]
    step = 0
    while (4 << step) < peers:
        got = xor_permute(mine_table, 4 << step)
        from_peer = (owners >> (2 + step)) == ((high >> step) ^ 1)
        mine_table = jnp.where(from_peer[:, None, None], got, mine_table)
        step += 1
    other_side = xor_permute(mine_table, 2)
    other_core = xor_permute(jnp.stack([mine_table, other_side]), 1)
    order = (
        (low, mine_table), (low ^ 2, other_side), (low ^ 3, other_core[1]), (low ^ 1, other_core[0])
    )
    heads = [h.astype(jnp.int32).reshape(1) for h, _ in order]
    first_block = (me * blocks).astype(jnp.int32).reshape(1)
    window = (first_block, queries, out_grad, halo, keys, values)
    stats = [window_stats(h, *window) for h in heads]
    parts = []
    for h, (_, table), stat in zip(heads, order, stats):
        table = table[None]
        parts.append(
            header_grads(
                h, links, queries, out_grad, table[..., :HEAD_SIZE], table[..., HEAD_SIZE:], stat
            )
        )
    arrived = [xor_permute(parts[at][2][0], mask) for at, mask in ((1, 2), (2, 3), (3, 1))]
    held = lax.optimization_barrier([(fin, dqt) for fin, dqt, _ in parts] + [parts[-1][2]])[:-1]
    grads = ()
    for h, (fin, dqt) in zip(heads, held):
        grads = window_grads(h, *window, fin, dqt, grads)
    query_grad, dk, dv, back = grads
    back = shifted(back, -1).astype(jnp.float32)
    total = parts[0][2][0].astype(jnp.float32)
    for x in arrived:
        total = total + x.astype(jnp.float32)
    while step > 0:
        step -= 1
        low_total = total.astype(jnp.bfloat16)
        total = total + xor_permute(low_total, 4 << step).astype(jnp.float32)
    wanted = owners[None, :] == (high * 4 + jnp.arange(4, dtype=jnp.int32))[:, None]
    owned = jnp.sum(
        jnp.where(wanted[:, :, None, None], total[None], 0.0), axis=1
    ).astype(jnp.bfloat16)
    owned = owned.reshape(2, 2, BLK, 2 * HEAD_SIZE)
    keep = pick(owned, side)
    got = xor_permute(pick(owned, 1 - side), 2)
    pair = jnp.where(side == 0, jnp.stack([keep, got]), jnp.stack([got, keep]))
    keep = lax.dynamic_index_in_dim(pair, core, 1, keepdims=False)
    give = lax.dynamic_index_in_dim(pair, 1 - core, 1, keepdims=False)
    got = xor_permute(give, 1)
    full = jnp.where(core == 0, jnp.stack([keep, got], axis=1), jnp.stack([got, keep], axis=1))
    full = full.reshape(KEY_VALUE_HEADS, BLK, 2 * HEAD_SIZE).astype(jnp.float32)

    def finish(grad, returned, own):
        grad = grad.at[rows - WIN :].add(returned)
        own = own.transpose(1, 0, 2).reshape(BLK, KEY_VALUE_HEADS * HEAD_SIZE)
        spread = (jnp.arange(blocks, dtype=jnp.int32) == offset) & jnp.any(mine)
        own = jnp.where(spread[:, None, None], own[None], 0.0)
        return grad + own.reshape(rows, KEY_VALUE_HEADS * HEAD_SIZE)

    return (
        query_grad,
        finish(dk, back[0], full[..., :HEAD_SIZE]),
        finish(dv, back[1], full[..., HEAD_SIZE:]),
    )


def solution(mesh):
    rows = P(("groups", "ctx"), None)
    return jax.shard_map(
        body,
        mesh=mesh,
        in_specs=(rows, rows, rows, rows, rows, P("groups")),
        out_specs=(rows, rows, rows),
        check_vma=False,
    )
```

```python
import functools

import jax
import jax.numpy as jnp
from jax import lax
from jax.experimental import pallas as pl
from jax.experimental.pallas import tpu as pltpu
from jax.sharding import PartitionSpec as P

QUERY_HEADS = 28
KEY_VALUE_HEADS = 4
HEAD_SIZE = 128
BLK = 128
WIN = 256
LINKS = 4
RATIO = QUERY_HEADS // KEY_VALUE_HEADS
LANES = RATIO * BLK
SPAN = WIN + BLK
FACTOR = float(HEAD_SIZE) ** (-0.5)
LOG2E = 1.4426950408889634
DEAD = -1e30
SCALE = FACTOR * LOG2E
STATS_MIB = 16
GRADS_MIB = 16
TILE = 16
FLIPS = (0, 2, 3, 1)
CHUNKS = tuple((at, min(at + 2, RATIO)) for at in range(0, RATIO, 2))

NT = (((1,), (1,)), ((), ()))
NN = (((1,), (0,)), ((), ()))


def dot(a, b, dims):
    return lax.dot_general(a, b, dims, preferred_element_type=jnp.float32)


def stacked(ref, lo, hi):
    return jnp.concatenate(
        [ref[:, r * HEAD_SIZE : (r + 1) * HEAD_SIZE] for r in range(lo, hi)], axis=0
    )


def extend(ext_ref, halo_ref, own_ref):
    ext_ref[0:WIN, :] = halo_ref[...]
    ext_ref[WIN:, :] = own_ref[...]


def dead_biases(block_id):
    first = jnp.where(block_id >= 2, 0.0, DEAD).astype(jnp.float32)
    mid = jnp.where(block_id >= 1, 0.0, DEAD).astype(jnp.float32)
    return first, mid


def queries_ahead(width):
    key_row = lax.broadcasted_iota(jnp.int32, (TILE, width), 0)
    query_row = lax.broadcasted_iota(jnp.int32, (TILE, width), 1) % BLK
    return query_row - key_row


def pair_scores(at, k, v, q_ref, g_ref, s_ref, da_ref):
    lo, hi = CHUNKS[at]
    width = (hi - lo) * BLK
    places = k.shape[0]
    s_ref[at % 2, 0:places, 0:width] = dot(k, stacked(q_ref, lo, hi), NT)
    da_ref[at % 2, 0:places, 0:width] = dot(v, stacked(g_ref, lo, hi), NT)


def window_stats_kernel(
    heads_ref, block_ref, q_ref, g_ref, k_halo, v_halo, k_own, v_own, *rest
):
    stat_ref, k_ext, v_ext, s_ref, da_ref = rest[-5:]
    b = pl.program_id(1)
    start = pl.multiple_of(b * BLK, BLK)

    @pl.when(b == 0)
    def _():
        extend(k_ext, k_halo, k_own)
        extend(v_ext, v_halo, v_own)

    first_bias, mid_bias = dead_biases(block_ref[0] + b)
    k = k_ext[pl.ds(start, SPAN), :]
    v = v_ext[pl.ds(start, SPAN), :]

    def stats(at):
        lo, hi = CHUNKS[at]
        width = (hi - lo) * BLK
        lanes = slice(lo * BLK, hi * BLK)
        s_at, da_at = s_ref.at[at % 2], da_ref.at[at % 2]
        ahead = queries_ahead(width)

        def tile(ref, row):
            return ref[row : row + TILE, 0:width]

        m = None
        m_mid = None
        for t in range(0, BLK, TILE):
            x = jnp.where(ahead >= t, tile(s_at, 2 * BLK + t), tile(s_at, t) + first_bias)
            s_at[2 * BLK + t : 2 * BLK + t + TILE, 0:width] = x
            m = x if m is None else jnp.maximum(m, x)
            x = tile(s_at, BLK + t)
            m_mid = x if m_mid is None else jnp.maximum(m_mid, x)
        m = jnp.maximum(m, m_mid + mid_bias)
        m = jnp.max(m, axis=0, keepdims=True) * SCALE
        m_mid = m - mid_bias
        l = jnp.zeros((TILE, width), jnp.float32)
        u = jnp.zeros((TILE, width), jnp.float32)
        for t in range(0, BLK, TILE):
            w = jnp.exp2(tile(s_at, 2 * BLK + t) * SCALE - m)
            da = jnp.where(ahead >= t, tile(da_at, 2 * BLK + t), tile(da_at, t))
            l = l + w
            u = u + w * da
            w = jnp.exp2(tile(s_at, BLK + t) * SCALE - m_mid)
            l = l + w
            u = u + w * tile(da_at, BLK + t)
        stat_ref[0:1, lanes] = m
        stat_ref[1:2, lanes] = jnp.sum(l, axis=0, keepdims=True)
        stat_ref[2:3, lanes] = jnp.sum(u, axis=0, keepdims=True)

    pair_scores(0, k, v, q_ref, g_ref, s_ref, da_ref)
    for at in range(len(CHUNKS)):
        if at + 1 < len(CHUNKS):
            pair_scores(at + 1, k, v, q_ref, g_ref, s_ref, da_ref)
        stats(at)


def header_kernel(
    heads_ref, links_ref, q_ref, g_ref, kh_ref, vh_ref, stat_ref, *rest
):
    fin_ref, dqt_ref, dkh_ref = rest[-10:-7]
    s_ref, da_ref, p_ref, ds_ref, dkh_acc, dvh_acc, ids_ref = rest[-7:]
    b = pl.program_id(1)
    last = pl.num_programs(1) - 1

    @pl.when(b == 0)
    def _():
        dkh_acc[...] = jnp.zeros_like(dkh_acc)
        dvh_acc[...] = jnp.zeros_like(dvh_acc)

    live = jnp.int32(0)
    for e in range(LINKS):
        entry = links_ref[b, e]

        @pl.when(entry >= 0)
        def _(entry=entry, live=live):
            ids_ref[live] = entry

        live = live + jnp.where(entry >= 0, 1, 0)

    @pl.when(live == 0)
    def _():
        l = stat_ref[1:2, :]
        fin_ref[0:1, :] = stat_ref[0:1, :] + jnp.log2(l)
        fin_ref[1:2, :] = stat_ref[2:3, :] / l
        dqt_ref[...] = jnp.zeros_like(dqt_ref)

    def block(count):
        ids = [ids_ref[j] for j in range(count)]
        k = jnp.concatenate([kh_ref[i] for i in ids], axis=0)
        v = jnp.concatenate([vh_ref[i] for i in ids], axis=0)
        places = count * BLK

        def weights(at):
            lo, hi = CHUNKS[at]
            width = (hi - lo) * BLK
            lanes = slice(lo * BLK, hi * BLK)
            s_at, da_at = s_ref.at[at % 2], da_ref.at[at % 2]

            def tile(ref, row):
                return ref[row : row + TILE, 0:width]

            m = tile(s_at, 0)
            for row in range(TILE, places, TILE):
                m = jnp.maximum(m, tile(s_at, row))
            before = stat_ref[0:1, lanes]
            m = jnp.maximum(before, jnp.max(m, axis=0, keepdims=True) * SCALE)
            l = jnp.zeros((TILE, width), jnp.float32)
            u = jnp.zeros((TILE, width), jnp.float32)
            for row in range(0, places, TILE):
                w = jnp.exp2(tile(s_at, row) * SCALE - m)
                s_at[row : row + TILE, 0:width] = w
                l = l + w
                u = u + w * tile(da_at, row)
            keep = jnp.exp2(before - m)
            l = jnp.sum(l, axis=0, keepdims=True) + keep * stat_ref[1:2, lanes]
            u = jnp.sum(u, axis=0, keepdims=True) + keep * stat_ref[2:3, lanes]
            inv = 1.0 / l
            delta = u * inv
            fin_ref[0:1, lanes] = m + jnp.log2(l)
            fin_ref[1:2, lanes] = delta
            for row in range(0, places, TILE):
                p = tile(s_at, row) * inv
                ds = p * (tile(da_at, row) - delta)
                p_ref[row : row + TILE, lanes] = p.astype(jnp.bfloat16)
                ds_ref[row : row + TILE, lanes] = ds.astype(jnp.bfloat16)

        pair_scores(0, k, v, q_ref, g_ref, s_ref, da_ref)
        for at in range(len(CHUNKS)):
            if at + 1 < len(CHUNKS):
                pair_scores(at + 1, k, v, q_ref, g_ref, s_ref, da_ref)
            weights(at)
        dqt_ref[...] = dot(k.T, ds_ref[0:places, :], NN)
        dk = dot(ds_ref[0:places, :], stacked(q_ref, 0, RATIO), NN)
        dv = dot(p_ref[0:places, :], stacked(g_ref, 0, RATIO), NN)
        for j, i in enumerate(ids):
            rows = slice(j * BLK, (j + 1) * BLK)
            dkh_acc[i] += dk[rows]
            dvh_acc[i] += dv[rows]

    for count in range(1, LINKS + 1):
        pl.when(live == count)(functools.partial(block, count))

    @pl.when(b == last)
    def _():
        dkh_ref[:, :, 0:HEAD_SIZE] = (dkh_acc[...] * FACTOR).astype(dkh_ref.dtype)
        dkh_ref[:, :, HEAD_SIZE:] = dvh_acc[...].astype(dkh_ref.dtype)


def window_grads_kernel(
    heads_ref, block_ref, q_ref, g_ref, k_halo, v_halo, k_own, v_own, fin_ref, dqt_ref, *rest
):
    (dq_ref, dk_ref, dv_ref, back_ref) = rest[-12:-8]
    (k_ext, v_ext, s_ref, da_ref, p_ref, ds_ref, dk_acc, dv_acc) = rest[-8:]
    b = pl.program_id(1)
    last = pl.num_programs(1) - 1
    start = pl.multiple_of(b * BLK, BLK)

    @pl.when(b == 0)
    def _():
        extend(k_ext, k_halo, k_own)
        extend(v_ext, v_halo, v_own)
        dk_acc[...] = jnp.zeros_like(dk_acc)
        dv_acc[...] = jnp.zeros_like(dv_acc)

    first_bias, mid_bias = dead_biases(block_ref[0] + b)
    k = k_ext[pl.ds(start, SPAN), :]
    v = v_ext[pl.ds(start, SPAN), :]

    def weights(at):
        lo, hi = CHUNKS[at]
        width = (hi - lo) * BLK
        lanes = slice(lo * BLK, hi * BLK)
        s_at, da_at = s_ref.at[at % 2], da_ref.at[at % 2]
        ahead = queries_ahead(width)
        top = fin_ref[0:1, lanes]
        delta = fin_ref[1:2, lanes]
        top_mid = top - mid_bias

        def tile(ref, row):
            return ref[row : row + TILE, 0:width]

        for t in range(0, BLK, TILE):
            own = ahead >= t
            s = jnp.where(own, tile(s_at, 2 * BLK + t), tile(s_at, t) + first_bias)
            da = jnp.where(own, tile(da_at, 2 * BLK + t), tile(da_at, t))
            p = jnp.exp2(s * SCALE - top)
            ds = p * (da - delta)
            for ref, x in ((p_ref, p), (ds_ref, ds)):
                ref[2 * BLK + t : 2 * BLK + t + TILE, lanes] = jnp.where(own, x, 0.0).astype(jnp.bfloat16)
                ref[t : t + TILE, lanes] = jnp.where(own, 0.0, x).astype(jnp.bfloat16)
            p = jnp.exp2(tile(s_at, BLK + t) * SCALE - top_mid)
            ds = p * (tile(da_at, BLK + t) - delta)
            p_ref[BLK + t : BLK + t + TILE, lanes] = p.astype(jnp.bfloat16)
            ds_ref[BLK + t : BLK + t + TILE, lanes] = ds.astype(jnp.bfloat16)

    pair_scores(0, k, v, q_ref, g_ref, s_ref, da_ref)
    for at in range(len(CHUNKS)):
        if at + 1 < len(CHUNKS):
            pair_scores(at + 1, k, v, q_ref, g_ref, s_ref, da_ref)
        weights(at)
    dqt = (dot(k.T, ds_ref[...], NN) + dqt_ref[...]) * FACTOR
    for r in range(RATIO):
        lanes = slice(r * BLK, (r + 1) * BLK)
        dq_ref[:, lanes] = dqt[:, lanes].astype(jnp.bfloat16).T
    dk_acc[pl.ds(start, SPAN), :] += dot(ds_ref[...], stacked(q_ref, 0, RATIO), NN)
    dv_acc[pl.ds(start, SPAN), :] += dot(p_ref[...], stacked(g_ref, 0, RATIO), NN)

    @pl.when(b == last)
    def _():
        dk_ref[...] = dk_acc[WIN:, :] * FACTOR
        dv_ref[...] = dv_acc[WIN:, :]
        back_ref[0] = (dk_acc[0:WIN, :] * FACTOR).astype(back_ref.dtype)
        back_ref[1] = dv_acc[0:WIN, :].astype(back_ref.dtype)


def own_offset(me, headers_ref, blocks, none):
    offset = jnp.int32(none)
    for l in range(headers_ref.shape[0]):
        block = headers_ref[l]
        offset = jnp.where(lax.div(block, blocks) == me, lax.rem(block, blocks), offset)
    return offset


def head_columns(low, flip):
    return pl.ds(pl.multiple_of(((low & 3) ^ flip) * HEAD_SIZE, HEAD_SIZE), HEAD_SIZE)


def pack_kernel(me_ref, headers_ref, k_ref, v_ref, keep_ref, give_ref, tail_ref):
    me = me_ref[0]
    rows = k_ref.shape[0]
    offset = own_offset(me, headers_ref, rows // BLK, 0)
    taken = pl.ds(pl.multiple_of(offset * BLK, BLK), BLK)
    for ref, at, flip in ((give_ref, 0, 1), (give_ref, 1, 3), (keep_ref, 0, 0), (keep_ref, 1, 2)):
        columns = head_columns(me, flip)
        ref[at, :, 0:HEAD_SIZE] = k_ref[taken, columns]
        ref[at, :, HEAD_SIZE:] = v_ref[taken, columns]
    width = k_ref.shape[1]
    tail_ref[:, 0:width] = k_ref[rows - WIN :, :]
    tail_ref[:, width:] = v_ref[rows - WIN :, :]


def whole_spec(x):
    return pl.BlockSpec(x.shape, functools.partial(lambda n, *_: (0,) * n, len(x.shape)))


def pack(me, header_blocks, keys, values):
    shapes = [jax.ShapeDtypeStruct((2, BLK, 2 * HEAD_SIZE), jnp.bfloat16)] * 2
    shapes.append(jax.ShapeDtypeStruct((WIN, 2 * keys.shape[1]), jnp.bfloat16))
    return pl.pallas_call(
        pack_kernel,
        grid_spec=pltpu.PrefetchScalarGridSpec(
            num_scalar_prefetch=2,
            grid=(1,),
            in_specs=[whole_spec(keys), whole_spec(values)],
            out_specs=[whole_spec(x) for x in shapes],
        ),
        out_shape=shapes,
    )(me, header_blocks, keys, values)


def window_specs(rows):
    wide = pl.BlockSpec((BLK, LANES), lambda i, b, h, *_: (b, h[0]))

    def column(rows, shift=0):
        return pl.BlockSpec((rows, HEAD_SIZE), lambda i, b, h, *_: (0, h[0] + shift))

    return wide, column(rows), [
        wide, wide, column(WIN), column(WIN, KEY_VALUE_HEADS), column(rows), column(rows)
    ]


def params(mebibytes):
    return pltpu.CompilerParams(
        dimension_semantics=("arbitrary", "arbitrary"), vmem_limit_bytes=mebibytes * 1024 * 1024
    )


def estimate(count, blocks, places, matmuls):
    flops = 2 * count * blocks * matmuls * places * LANES * HEAD_SIZE
    return pl.CostEstimate(
        flops=flops, bytes_accessed=count * blocks * BLK * LANES * 6, transcendentals=0
    )


def pair_scratch(places):
    return [pltpu.VMEM((2, places, 2 * BLK), jnp.float32)] * 2


def block_spec(rows):
    return pl.BlockSpec((None, rows, LANES), lambda i, b, *_: (b, 0, 0))


def window_stats(head, first_block, queries, out_grad, halo, keys, values):
    rows = queries.shape[0]
    blocks = rows // BLK
    return pl.pallas_call(
        window_stats_kernel,
        grid_spec=pltpu.PrefetchScalarGridSpec(
            num_scalar_prefetch=2,
            grid=(1, blocks),
            in_specs=window_specs(rows)[2],
            out_specs=block_spec(8),
            scratch_shapes=[pltpu.VMEM((WIN + rows, HEAD_SIZE), jnp.bfloat16)] * 2
            + pair_scratch(SPAN),
        ),
        out_shape=jax.ShapeDtypeStruct((blocks, 8, LANES), jnp.float32),
        compiler_params=params(STATS_MIB),
        cost_estimate=estimate(1, blocks, SPAN, 5),
    )(head, first_block, queries, out_grad, halo, halo, keys, values)


def header_grads(head, links, queries, out_grad, table, stats):
    headers = table.shape[0]
    blocks = queries.shape[0] // BLK
    wide = pl.BlockSpec((BLK, LANES), lambda i, b, h, *_: (b, h[0]))
    half = pl.BlockSpec((headers, BLK, HEAD_SIZE), lambda i, b, *_: (0, 0, 0))
    other_half = pl.BlockSpec((headers, BLK, HEAD_SIZE), lambda i, b, *_: (0, 0, 1))
    whole = pl.BlockSpec((headers, BLK, 2 * HEAD_SIZE), lambda i, b, *_: (0, 0, 0))
    return pl.pallas_call(
        header_kernel,
        grid_spec=pltpu.PrefetchScalarGridSpec(
            num_scalar_prefetch=2,
            grid=(1, blocks),
            in_specs=[wide, wide, half, other_half, block_spec(8)],
            out_specs=[block_spec(8), block_spec(HEAD_SIZE), whole],
            scratch_shapes=pair_scratch(LINKS * BLK)
            + [pltpu.VMEM((LINKS * BLK, LANES), jnp.bfloat16)] * 2
            + [pltpu.VMEM((headers, BLK, HEAD_SIZE), jnp.float32)] * 2
            + [pltpu.SMEM((LINKS,), jnp.int32)],
        ),
        out_shape=[
            jax.ShapeDtypeStruct((blocks, 8, LANES), jnp.float32),
            jax.ShapeDtypeStruct((blocks, HEAD_SIZE, LANES), jnp.float32),
            jax.ShapeDtypeStruct(table.shape, jnp.bfloat16),
        ],
        compiler_params=params(GRADS_MIB),
        cost_estimate=estimate(1, blocks, 3 * BLK, 7),
    )(head, links, queries, out_grad, table, table, stats)


def window_grads(head, first_block, queries, out_grad, halo, keys, values, fin, dqt, carried):
    rows = queries.shape[0]
    blocks = rows // BLK
    wide, column, specs = window_specs(rows)
    carried = tuple(carried)
    alone = len(carried) == 3
    first = 2 + len(specs) + 2
    return pl.pallas_call(
        window_grads_kernel,
        grid_spec=pltpu.PrefetchScalarGridSpec(
            num_scalar_prefetch=2,
            grid=(1, blocks),
            in_specs=specs
            + [block_spec(8), block_spec(HEAD_SIZE)]
            + [pl.BlockSpec(memory_space=pl.ANY)] * len(carried),
            out_specs=[
                wide, column, column,
                pl.BlockSpec((2, WIN, HEAD_SIZE), lambda i, b, h, *_: (0, 0, 0 if alone else h[0])),
            ],
            scratch_shapes=[pltpu.VMEM((WIN + rows, HEAD_SIZE), jnp.bfloat16)] * 2
            + pair_scratch(SPAN)
            + [pltpu.VMEM((SPAN, LANES), jnp.bfloat16)] * 2
            + [pltpu.VMEM((WIN + rows, HEAD_SIZE), jnp.float32)] * 2,
        ),
        out_shape=[
            jax.ShapeDtypeStruct(queries.shape, jnp.bfloat16),
            jax.ShapeDtypeStruct(keys.shape, jnp.float32),
            jax.ShapeDtypeStruct(values.shape, jnp.float32),
            jax.ShapeDtypeStruct((2, WIN, HEAD_SIZE if alone else keys.shape[1]), jnp.bfloat16),
        ],
        input_output_aliases={first + i: i for i in range(len(carried))},
        compiler_params=params(GRADS_MIB),
        cost_estimate=estimate(1, blocks, SPAN, 8),
    )(head, first_block, queries, out_grad, halo, halo, keys, values, fin, dqt, *carried)


def xor_permute(x, mask):
    peers = lax.axis_size("ctx")
    return lax.ppermute(x, "ctx", [(i, i ^ mask) for i in range(peers)])


def shifted(x, by):
    peers = lax.axis_size("ctx")
    pairs = [(i, i + by) for i in range(peers) if 0 <= i + by < peers]
    return lax.ppermute(x, "ctx", pairs)


def body(queries, keys, values, out_grad, links, header_blocks):
    rows = queries.shape[0]
    blocks = rows // BLK
    peers = lax.axis_size("ctx")
    me = lax.axis_index("ctx")
    low = me & 3
    heads = [(low ^ flip).astype(jnp.int32).reshape(1) for flip in FLIPS]
    first_block = (me * blocks).astype(jnp.int32).reshape(1)
    device = me.astype(jnp.int32).reshape(1)

    keep, give, tail = pack(device, header_blocks, keys, values)
    got = xor_permute(give, 1)
    far_heads = jnp.stack([keep[1], got[1]])
    barrier = lax.optimization_barrier
    far_heads, tail, me, header_blocks = barrier((far_heads, tail, me, header_blocks))
    side = xor_permute(far_heads, 2)
    halo = shifted(tail, 1)
    low = me & 3
    high = me >> 2
    owners = header_blocks // blocks
    near = jnp.stack([keep[0], got[0], side[0], side[1]])
    table = near[(owners ^ me) & 3]

    window = (first_block, queries, out_grad, halo, keys, values)
    stats = []
    step = 0
    while (4 << step) < peers:
        got = xor_permute(table, 4 << step)
        if len(stats) < KEY_VALUE_HEADS:
            until = 1 if step == 0 else KEY_VALUE_HEADS
            pair = [window_stats(h, *window) for h in heads[len(stats) : until]]
            got, pair = barrier((got, pair))
            stats += pair
        from_peer = (owners >> (2 + step)) == ((high >> step) ^ 1)
        table = jnp.where(from_peer[:, None, None], got, table)
        step += 1
    stats += [window_stats(h, *window) for h in heads[len(stats) :]]

    def header_part(at, table):
        return header_grads(heads[at], links, queries, out_grad, table, stats[at])

    def window_part(at, fin, carried):
        return window_grads(heads[at], *window, *fin, carried)

    other_side = xor_permute(table, 2)
    *fin0, own_sum = header_part(0, table)
    other_side, own_sum = barrier((other_side, own_sum))
    other_core = xor_permute(jnp.stack([other_side, table]), 1)
    *fin1, side_sum = header_part(1, other_side)
    arrived = [xor_permute(side_sum, 2)]
    *fin2, far_sum = header_part(2, other_core[0])
    arrived.append(xor_permute(far_sum, 3))
    *fin3, core_sum = header_part(3, other_core[1])
    arrived.append(xor_permute(core_sum, 1))

    fin0, core_sum = barrier((fin0, core_sum))
    query_grad, dk, dv, back = window_part(0, fin0, ())
    total = own_sum.astype(jnp.float32)
    arrived, query_grad = barrier((arrived, query_grad))
    for x in arrived:
        total = total + x.astype(jnp.float32)
    step -= 1
    sent, query_grad = barrier((total.astype(jnp.bfloat16), query_grad))
    got = xor_permute(sent, 4 << step)
    query_grad, dk, dv, back = window_part(1, fin1, (query_grad, dk, dv, back))
    query_grad, dk, dv, back = window_part(2, fin2, (query_grad, dk, dv, back))
    back = shifted(back, -1)
    got, query_grad = barrier((got, query_grad))
    total = total + got.astype(jnp.float32)
    while step > 1:
        step -= 1
        total = total + xor_permute(total.astype(jnp.bfloat16), 4 << step).astype(jnp.float32)
    sent, query_grad = barrier((total.astype(jnp.bfloat16), query_grad))
    got = xor_permute(sent, 4)
    query_grad, dk, dv, last_back = window_part(3, fin3, (query_grad, dk, dv))
    got, last_back = barrier((got, last_back))
    total = total + got.astype(jnp.float32)

    group = me ^ jnp.arange(4, dtype=jnp.int32)
    wanted = owners[None, :] == group[:, None]
    owned = jnp.sum(jnp.where(wanted[:, :, None, None], total[None], 0.0), axis=1).astype(jnp.bfloat16)
    owned, last_back = barrier((owned, last_back))
    side = xor_permute(owned[2:], 2)
    last_back = shifted(last_back, -1)
    far = xor_permute(jnp.stack([owned[1], side[1]]), 1)

    last_head = ((me + 1) & 3) ^ FLIPS[-1]
    column = jnp.arange(keys.shape[1], dtype=jnp.int32) // HEAD_SIZE
    last_back = jnp.concatenate([last_back] * KEY_VALUE_HEADS, axis=2)
    back = jnp.where(column == last_head, last_back, back).astype(jnp.float32)
    parts = (owned[0], far[0], side[0], far[1])
    offset = jnp.sum(jnp.where(owners == me, header_blocks % blocks + 1, 0)) - 1

    def summed(grad, returned, columns):
        own = []
        for head in range(KEY_VALUE_HEADS):
            x = parts[head ^ 3]
            for other in range(3):
                x = jnp.where(low == other, parts[head ^ other], x)
            own.append(x[:, columns].astype(jnp.float32))
        own = jnp.concatenate(own, axis=1)
        pieces = []
        for block in range(blocks):
            piece = grad[block * BLK : (block + 1) * BLK]
            at = block * BLK - (rows - WIN)
            if at >= 0:
                piece = piece + returned[at : at + BLK]
            pieces.append(piece + jnp.where(offset == block, own, 0.0))
        return jnp.concatenate(pieces, axis=0)

    dk = summed(dk, back[0], slice(0, HEAD_SIZE))
    dv = summed(dv, back[1], slice(HEAD_SIZE, 2 * HEAD_SIZE))
    return query_grad, dk, dv


def solution(mesh):
    rows = P(("groups", "ctx"), None)
    return jax.shard_map(
        body,
        mesh=mesh,
        in_specs=(rows, rows, rows, rows, rows, P("groups")),
        out_specs=(rows, rows, rows),
        check_vma=False,
    )
```

```python
import functools

import jax
import jax.numpy as jnp
from jax import lax
from jax.experimental import pallas as pl
from jax.experimental.pallas import tpu as pltpu
from jax.sharding import PartitionSpec as P

QUERY_HEADS = 28
KEY_VALUE_HEADS = 4
HEAD_SIZE = 128
BLK = 128
WIN = 256
LINKS = 4
RATIO = QUERY_HEADS // KEY_VALUE_HEADS
LANES = RATIO * BLK
SPAN = WIN + BLK
FACTOR = float(HEAD_SIZE) ** (-0.5)
LOG2E = 1.4426950408889634
DEAD = -1e30
SCALE = FACTOR * LOG2E
ALL, FIRST, REST = range(3)
STATS_MIB = 16
GRADS_MIB = 16
TILE = 16
FLIPS = (0, 2, 3, 1)
CHUNKS = tuple((at, min(at + 2, RATIO)) for at in range(0, RATIO, 2))

NT = (((1,), (1,)), ((), ()))
NN = (((1,), (0,)), ((), ()))


def dot(a, b, dims):
    return lax.dot_general(a, b, dims, preferred_element_type=jnp.float32)


def stacked(ref, lo, hi):
    return jnp.concatenate(
        [ref[:, r * HEAD_SIZE : (r + 1) * HEAD_SIZE] for r in range(lo, hi)], axis=0
    )


def extend(ext_ref, halo_ref, own_ref):
    ext_ref[0:WIN, :] = halo_ref[...]
    ext_ref[WIN:, :] = own_ref[...]


def dead_biases(block_id):
    first = jnp.where(block_id >= 2, 0.0, DEAD).astype(jnp.float32)
    mid = jnp.where(block_id >= 1, 0.0, DEAD).astype(jnp.float32)
    return first, mid


def queries_ahead(width):
    key_row = lax.broadcasted_iota(jnp.int32, (TILE, width), 0)
    query_row = lax.broadcasted_iota(jnp.int32, (TILE, width), 1) % BLK
    return query_row - key_row


def pair_scores(at, k, v, q_ref, g_ref, s_ref, da_ref):
    lo, hi = CHUNKS[at]
    width = (hi - lo) * BLK
    places = k.shape[0]
    s_ref[at % 2, 0:places, 0:width] = dot(k, stacked(q_ref, lo, hi), NT)
    da_ref[at % 2, 0:places, 0:width] = dot(v, stacked(g_ref, lo, hi), NT)


def window_stats_kernel(
    heads_ref, block_ref, q_ref, g_ref, k_halo, v_halo, k_own, v_own, *rest
):
    stat_ref, k_ext, v_ext, s_ref, da_ref = rest[-5:]
    b = pl.program_id(1)
    start = pl.multiple_of(b * BLK, BLK)

    @pl.when(b == 0)
    def _():
        extend(k_ext, k_halo, k_own)
        extend(v_ext, v_halo, v_own)

    first_bias, mid_bias = dead_biases(block_ref[0] + b)
    k = k_ext[pl.ds(start, SPAN), :]
    v = v_ext[pl.ds(start, SPAN), :]

    def stats(at):
        lo, hi = CHUNKS[at]
        width = (hi - lo) * BLK
        lanes = slice(lo * BLK, hi * BLK)
        s_at, da_at = s_ref.at[at % 2], da_ref.at[at % 2]
        ahead = queries_ahead(width)

        def tile(ref, row):
            return ref[row : row + TILE, 0:width]

        m = None
        m_mid = None
        for t in range(0, BLK, TILE):
            x = jnp.where(ahead >= t, tile(s_at, 2 * BLK + t), tile(s_at, t) + first_bias)
            s_at[2 * BLK + t : 2 * BLK + t + TILE, 0:width] = x
            m = x if m is None else jnp.maximum(m, x)
            x = tile(s_at, BLK + t)
            m_mid = x if m_mid is None else jnp.maximum(m_mid, x)
        m = jnp.maximum(m, m_mid + mid_bias)
        m = jnp.max(m, axis=0, keepdims=True) * SCALE
        m_mid = m - mid_bias
        l = jnp.zeros((TILE, width), jnp.float32)
        u = jnp.zeros((TILE, width), jnp.float32)
        for t in range(0, BLK, TILE):
            w = jnp.exp2(tile(s_at, 2 * BLK + t) * SCALE - m)
            da = jnp.where(ahead >= t, tile(da_at, 2 * BLK + t), tile(da_at, t))
            l = l + w
            u = u + w * da
            w = jnp.exp2(tile(s_at, BLK + t) * SCALE - m_mid)
            l = l + w
            u = u + w * tile(da_at, BLK + t)
        stat_ref[0:1, lanes] = m
        stat_ref[1:2, lanes] = jnp.sum(l, axis=0, keepdims=True)
        stat_ref[2:3, lanes] = jnp.sum(u, axis=0, keepdims=True)

    pair_scores(0, k, v, q_ref, g_ref, s_ref, da_ref)
    for at in range(len(CHUNKS)):
        if at + 1 < len(CHUNKS):
            pair_scores(at + 1, k, v, q_ref, g_ref, s_ref, da_ref)
        stats(at)


def header_kernel(
    heads_ref, links_ref, q_ref, g_ref, kh_ref, vh_ref, stat_ref, *rest
):
    fin_ref, dqt_ref, dkh_ref = rest[-10:-7]
    s_ref, da_ref, p_ref, ds_ref, dkh_acc, dvh_acc, ids_ref = rest[-7:]
    b = pl.program_id(1)
    last = pl.num_programs(1) - 1

    @pl.when(b == 0)
    def _():
        dkh_acc[...] = jnp.zeros_like(dkh_acc)
        dvh_acc[...] = jnp.zeros_like(dvh_acc)

    live = jnp.int32(0)
    for e in range(LINKS):
        entry = links_ref[b, e]

        @pl.when(entry >= 0)
        def _(entry=entry, live=live):
            ids_ref[live] = entry

        live = live + jnp.where(entry >= 0, 1, 0)

    @pl.when(live == 0)
    def _():
        l = stat_ref[1:2, :]
        fin_ref[0:1, :] = stat_ref[0:1, :] + jnp.log2(l)
        fin_ref[1:2, :] = stat_ref[2:3, :] / l
        dqt_ref[...] = jnp.zeros_like(dqt_ref)

    def block(count):
        ids = [ids_ref[j] for j in range(count)]
        k = jnp.concatenate([kh_ref[i] for i in ids], axis=0)
        v = jnp.concatenate([vh_ref[i] for i in ids], axis=0)
        places = count * BLK

        def weights(at):
            lo, hi = CHUNKS[at]
            width = (hi - lo) * BLK
            lanes = slice(lo * BLK, hi * BLK)
            s_at, da_at = s_ref.at[at % 2], da_ref.at[at % 2]

            def tile(ref, row):
                return ref[row : row + TILE, 0:width]

            m = tile(s_at, 0)
            for row in range(TILE, places, TILE):
                m = jnp.maximum(m, tile(s_at, row))
            before = stat_ref[0:1, lanes]
            m = jnp.maximum(before, jnp.max(m, axis=0, keepdims=True) * SCALE)
            l = jnp.zeros((TILE, width), jnp.float32)
            u = jnp.zeros((TILE, width), jnp.float32)
            for row in range(0, places, TILE):
                w = jnp.exp2(tile(s_at, row) * SCALE - m)
                s_at[row : row + TILE, 0:width] = w
                l = l + w
                u = u + w * tile(da_at, row)
            keep = jnp.exp2(before - m)
            l = jnp.sum(l, axis=0, keepdims=True) + keep * stat_ref[1:2, lanes]
            u = jnp.sum(u, axis=0, keepdims=True) + keep * stat_ref[2:3, lanes]
            inv = 1.0 / l
            delta = u * inv
            fin_ref[0:1, lanes] = m + jnp.log2(l)
            fin_ref[1:2, lanes] = delta
            for row in range(0, places, TILE):
                p = tile(s_at, row) * inv
                ds = p * (tile(da_at, row) - delta)
                p_ref[row : row + TILE, lanes] = p.astype(jnp.bfloat16)
                ds_ref[row : row + TILE, lanes] = ds.astype(jnp.bfloat16)

        pair_scores(0, k, v, q_ref, g_ref, s_ref, da_ref)
        for at in range(len(CHUNKS)):
            if at + 1 < len(CHUNKS):
                pair_scores(at + 1, k, v, q_ref, g_ref, s_ref, da_ref)
            weights(at)
        dqt_ref[...] = dot(k.T, ds_ref[0:places, :], NN)
        dk = dot(ds_ref[0:places, :], stacked(q_ref, 0, RATIO), NN)
        dv = dot(p_ref[0:places, :], stacked(g_ref, 0, RATIO), NN)
        for j, i in enumerate(ids):
            rows = slice(j * BLK, (j + 1) * BLK)
            dkh_acc[i] += dk[rows]
            dvh_acc[i] += dv[rows]

    for count in range(1, LINKS + 1):
        pl.when(live == count)(functools.partial(block, count))

    @pl.when(b == last)
    def _():
        dkh_ref[:, :, 0:HEAD_SIZE] = (dkh_acc[...] * FACTOR).astype(dkh_ref.dtype)
        dkh_ref[:, :, HEAD_SIZE:] = dvh_acc[...].astype(dkh_ref.dtype)


def window_grads_kernel(
    stage, heads_ref, block_ref, q_ref, g_ref, k_halo, v_halo, k_own, v_own, fin_ref, dqt_ref, *rest
):
    (k_ext, v_ext, s_ref, da_ref, p_ref, ds_ref, dk_acc, dv_acc) = rest[-8:]
    if stage == FIRST:
        dq_ref, back_ref, part_ref = rest[-11:-8]
    elif stage == REST:
        part_ref = rest[0]
        dq_ref, dk_ref, dv_ref = rest[-11:-8]
    else:
        dq_ref, back_ref, dk_ref, dv_ref = rest[-12:-8]
    step = pl.program_id(1)
    last = pl.num_programs(1) - 1
    b = step + WIN // BLK if stage == REST else step
    start = pl.multiple_of(b * BLK, BLK)

    @pl.when(step == 0)
    def _():
        extend(k_ext, k_halo, k_own)
        extend(v_ext, v_halo, v_own)
        dk_acc[...] = jnp.zeros_like(dk_acc)
        dv_acc[...] = jnp.zeros_like(dv_acc)
        if stage == REST:
            dk_acc[WIN : 2 * WIN, :] = part_ref[0]
            dv_acc[WIN : 2 * WIN, :] = part_ref[1]

    first_bias, mid_bias = dead_biases(block_ref[0] + b)
    k = k_ext[pl.ds(start, SPAN), :]
    v = v_ext[pl.ds(start, SPAN), :]

    def weights(at):
        lo, hi = CHUNKS[at]
        width = (hi - lo) * BLK
        lanes = slice(lo * BLK, hi * BLK)
        s_at, da_at = s_ref.at[at % 2], da_ref.at[at % 2]
        ahead = queries_ahead(width)
        top = fin_ref[0:1, lanes]
        delta = fin_ref[1:2, lanes]
        top_mid = top - mid_bias

        def tile(ref, row):
            return ref[row : row + TILE, 0:width]

        for t in range(0, BLK, TILE):
            own = ahead >= t
            s = jnp.where(own, tile(s_at, 2 * BLK + t), tile(s_at, t) + first_bias)
            da = jnp.where(own, tile(da_at, 2 * BLK + t), tile(da_at, t))
            p = jnp.exp2(s * SCALE - top)
            ds = p * (da - delta)
            for ref, x in ((p_ref, p), (ds_ref, ds)):
                ref[2 * BLK + t : 2 * BLK + t + TILE, lanes] = jnp.where(own, x, 0.0).astype(jnp.bfloat16)
                ref[t : t + TILE, lanes] = jnp.where(own, 0.0, x).astype(jnp.bfloat16)
            p = jnp.exp2(tile(s_at, BLK + t) * SCALE - top_mid)
            ds = p * (tile(da_at, BLK + t) - delta)
            p_ref[BLK + t : BLK + t + TILE, lanes] = p.astype(jnp.bfloat16)
            ds_ref[BLK + t : BLK + t + TILE, lanes] = ds.astype(jnp.bfloat16)

    pair_scores(0, k, v, q_ref, g_ref, s_ref, da_ref)
    for at in range(len(CHUNKS)):
        if at + 1 < len(CHUNKS):
            pair_scores(at + 1, k, v, q_ref, g_ref, s_ref, da_ref)
        weights(at)
    dqt = (dot(k.T, ds_ref[...], NN) + dqt_ref[...]) * FACTOR
    for r in range(RATIO):
        lanes = slice(r * BLK, (r + 1) * BLK)
        dq_ref[:, lanes] = dqt[:, lanes].astype(jnp.bfloat16).T
    dk_acc[pl.ds(start, SPAN), :] += dot(ds_ref[...], stacked(q_ref, 0, RATIO), NN)
    dv_acc[pl.ds(start, SPAN), :] += dot(p_ref[...], stacked(g_ref, 0, RATIO), NN)

    @pl.when(step == last)
    def _():
        if stage != REST:
            back_ref[0] = (dk_acc[0:WIN, :] * FACTOR).astype(back_ref.dtype)
            back_ref[1] = dv_acc[0:WIN, :].astype(back_ref.dtype)
        if stage == FIRST:
            part_ref[0] = dk_acc[WIN : 2 * WIN, :]
            part_ref[1] = dv_acc[WIN : 2 * WIN, :]
        else:
            dk_ref[...] = dk_acc[WIN:, :] * FACTOR
            dv_ref[...] = dv_acc[WIN:, :]


def own_offset(me, headers_ref, blocks, none):
    offset = jnp.int32(none)
    for l in range(headers_ref.shape[0]):
        block = headers_ref[l]
        offset = jnp.where(lax.div(block, blocks) == me, lax.rem(block, blocks), offset)
    return offset


def head_columns(low, flip):
    return pl.ds(pl.multiple_of(((low & 3) ^ flip) * HEAD_SIZE, HEAD_SIZE), HEAD_SIZE)


def pack_kernel(me_ref, headers_ref, k_ref, v_ref, keep_ref, give_ref, tail_ref):
    me = me_ref[0]
    rows = k_ref.shape[0]
    offset = own_offset(me, headers_ref, rows // BLK, 0)
    taken = pl.ds(pl.multiple_of(offset * BLK, BLK), BLK)
    for ref, at, flip in ((give_ref, 0, 1), (give_ref, 1, 3), (keep_ref, 0, 0), (keep_ref, 1, 2)):
        columns = head_columns(me, flip)
        ref[at, :, 0:HEAD_SIZE] = k_ref[taken, columns]
        ref[at, :, HEAD_SIZE:] = v_ref[taken, columns]
    width = k_ref.shape[1]
    tail_ref[:, 0:width] = k_ref[rows - WIN :, :]
    tail_ref[:, width:] = v_ref[rows - WIN :, :]


def whole_spec(x):
    return pl.BlockSpec(x.shape, functools.partial(lambda n, *_: (0,) * n, len(x.shape)))


def pack(me, header_blocks, keys, values):
    shapes = [jax.ShapeDtypeStruct((2, BLK, 2 * HEAD_SIZE), jnp.bfloat16)] * 2
    shapes.append(jax.ShapeDtypeStruct((WIN, 2 * keys.shape[1]), jnp.bfloat16))
    return pl.pallas_call(
        pack_kernel,
        grid_spec=pltpu.PrefetchScalarGridSpec(
            num_scalar_prefetch=2,
            grid=(1,),
            in_specs=[whole_spec(keys), whole_spec(values)],
            out_specs=[whole_spec(x) for x in shapes],
        ),
        out_shape=shapes,
    )(me, header_blocks, keys, values)


def window_specs(rows):
    wide = pl.BlockSpec((BLK, LANES), lambda i, b, h, *_: (b, h[0]))

    def column(rows, shift=0):
        return pl.BlockSpec((rows, HEAD_SIZE), lambda i, b, h, *_: (0, h[0] + shift))

    return wide, column(rows), [
        wide, wide, column(WIN), column(WIN, KEY_VALUE_HEADS), column(rows), column(rows)
    ]


def params(mebibytes):
    return pltpu.CompilerParams(
        dimension_semantics=("arbitrary", "arbitrary"), vmem_limit_bytes=mebibytes * 1024 * 1024
    )


def estimate(count, blocks, places, matmuls):
    flops = 2 * count * blocks * matmuls * places * LANES * HEAD_SIZE
    return pl.CostEstimate(
        flops=flops, bytes_accessed=count * blocks * BLK * LANES * 6, transcendentals=0
    )


def pair_scratch(places):
    return [pltpu.VMEM((2, places, 2 * BLK), jnp.float32)] * 2


def block_spec(rows):
    return pl.BlockSpec((None, rows, LANES), lambda i, b, *_: (b, 0, 0))


def window_stats(head, first_block, queries, out_grad, halo, keys, values):
    rows = queries.shape[0]
    blocks = rows // BLK
    return pl.pallas_call(
        window_stats_kernel,
        grid_spec=pltpu.PrefetchScalarGridSpec(
            num_scalar_prefetch=2,
            grid=(1, blocks),
            in_specs=window_specs(rows)[2],
            out_specs=block_spec(8),
            scratch_shapes=[pltpu.VMEM((WIN + rows, HEAD_SIZE), jnp.bfloat16)] * 2
            + pair_scratch(SPAN),
        ),
        out_shape=jax.ShapeDtypeStruct((blocks, 8, LANES), jnp.float32),
        compiler_params=params(STATS_MIB),
        cost_estimate=estimate(1, blocks, SPAN, 5),
    )(head, first_block, queries, out_grad, halo, halo, keys, values)


def header_grads(head, links, queries, out_grad, table, stats):
    headers = table.shape[0]
    blocks = queries.shape[0] // BLK
    wide = pl.BlockSpec((BLK, LANES), lambda i, b, h, *_: (b, h[0]))
    half = pl.BlockSpec((headers, BLK, HEAD_SIZE), lambda i, b, *_: (0, 0, 0))
    other_half = pl.BlockSpec((headers, BLK, HEAD_SIZE), lambda i, b, *_: (0, 0, 1))
    whole = pl.BlockSpec((headers, BLK, 2 * HEAD_SIZE), lambda i, b, *_: (0, 0, 0))
    return pl.pallas_call(
        header_kernel,
        grid_spec=pltpu.PrefetchScalarGridSpec(
            num_scalar_prefetch=2,
            grid=(1, blocks),
            in_specs=[wide, wide, half, other_half, block_spec(8)],
            out_specs=[block_spec(8), block_spec(HEAD_SIZE), whole],
            scratch_shapes=pair_scratch(LINKS * BLK)
            + [pltpu.VMEM((LINKS * BLK, LANES), jnp.bfloat16)] * 2
            + [pltpu.VMEM((headers, BLK, HEAD_SIZE), jnp.float32)] * 2
            + [pltpu.SMEM((LINKS,), jnp.int32)],
        ),
        out_shape=[
            jax.ShapeDtypeStruct((blocks, 8, LANES), jnp.float32),
            jax.ShapeDtypeStruct((blocks, HEAD_SIZE, LANES), jnp.float32),
            jax.ShapeDtypeStruct(table.shape, jnp.bfloat16),
        ],
        compiler_params=params(GRADS_MIB),
        cost_estimate=estimate(1, blocks, 3 * BLK, 7),
    )(head, links, queries, out_grad, table, table, stats)


def window_grads(stage, head, first_block, queries, out_grad, halo, keys, values, fin, dqt, part, carried):
    rows, width = keys.shape
    blocks = rows // BLK
    halo_blocks = WIN // BLK
    at = halo_blocks if stage == REST else 0
    steps = {FIRST: halo_blocks, REST: blocks - halo_blocks, ALL: blocks}[stage]
    wide = pl.BlockSpec((BLK, LANES), lambda i, b, h, *_: (b + at, h[0]))
    column = window_specs(rows)[1]
    back = pl.BlockSpec((2, WIN, HEAD_SIZE), lambda i, b, h, *_: (0, 0, h[0]))
    own_part = pl.BlockSpec((2, WIN, HEAD_SIZE), lambda i, b, *_: (0, 0, 0))
    specs = [wide, wide] + window_specs(rows)[2][2:] + [
        pl.BlockSpec((None, n, LANES), lambda i, b, *_: (b + at, 0, 0)) for n in (8, HEAD_SIZE)
    ]
    operands = [queries, out_grad, halo, halo, keys, values, fin, dqt]
    dq_shape = jax.ShapeDtypeStruct(queries.shape, jnp.bfloat16)
    back_shape = jax.ShapeDtypeStruct((2, WIN, width), jnp.bfloat16)
    sums = [jax.ShapeDtypeStruct(keys.shape, jnp.float32)] * 2
    if stage == FIRST:
        shapes = [dq_shape, back_shape, jax.ShapeDtypeStruct((2, WIN, HEAD_SIZE), jnp.float32)]
        out_specs = [wide, back, own_part]
    elif stage == REST:
        specs.append(own_part)
        operands.append(part)
        shapes = [dq_shape] + sums
        out_specs = [wide, column, column]
    else:
        shapes = [dq_shape, back_shape] + sums
        out_specs = [wide, back, column, column]
    first = 2 + len(specs)
    return pl.pallas_call(
        functools.partial(window_grads_kernel, stage),
        grid_spec=pltpu.PrefetchScalarGridSpec(
            num_scalar_prefetch=2,
            grid=(1, steps),
            in_specs=specs + [pl.BlockSpec(memory_space=pl.ANY)] * len(carried),
            out_specs=out_specs,
            scratch_shapes=[pltpu.VMEM((WIN + rows, HEAD_SIZE), jnp.bfloat16)] * 2
            + pair_scratch(SPAN)
            + [pltpu.VMEM((SPAN, LANES), jnp.bfloat16)] * 2
            + [pltpu.VMEM((WIN + rows, HEAD_SIZE), jnp.float32)] * 2,
        ),
        out_shape=shapes,
        input_output_aliases={first + i: out for i, out in enumerate(carried)},
        compiler_params=params(GRADS_MIB),
        cost_estimate=estimate(1, steps, SPAN, 8),
    )(head, first_block, *operands, *carried.values())


def xor_permute(x, mask):
    peers = lax.axis_size("ctx")
    return lax.ppermute(x, "ctx", [(i, i ^ mask) for i in range(peers)])


def shifted(x, by):
    peers = lax.axis_size("ctx")
    pairs = [(i, i + by) for i in range(peers) if 0 <= i + by < peers]
    return lax.ppermute(x, "ctx", pairs)


def body(queries, keys, values, out_grad, links, header_blocks):
    rows = queries.shape[0]
    blocks = rows // BLK
    peers = lax.axis_size("ctx")
    me = lax.axis_index("ctx")
    low = me & 3
    heads = [(low ^ flip).astype(jnp.int32).reshape(1) for flip in FLIPS]
    first_block = (me * blocks).astype(jnp.int32).reshape(1)
    device = me.astype(jnp.int32).reshape(1)

    keep, give, tail = pack(device, header_blocks, keys, values)
    got = xor_permute(give, 1)
    far_heads = jnp.stack([keep[1], got[1]])
    barrier = lax.optimization_barrier
    far_heads, tail, me, header_blocks = barrier((far_heads, tail, me, header_blocks))
    side = xor_permute(far_heads, 2)
    halo = shifted(tail, 1)
    low = me & 3
    high = me >> 2
    owners = header_blocks // blocks
    near = jnp.stack([keep[0], got[0], side[0], side[1]])
    table = near[(owners ^ me) & 3]

    window = (first_block, queries, out_grad, halo, keys, values)
    stats = []
    step = 0
    while (4 << step) < peers:
        got = xor_permute(table, 4 << step)
        if len(stats) < KEY_VALUE_HEADS:
            until = 1 if step == 0 else KEY_VALUE_HEADS
            pair = [window_stats(h, *window) for h in heads[len(stats) : until]]
            got, pair = barrier((got, pair))
            stats += pair
        from_peer = (owners >> (2 + step)) == ((high >> step) ^ 1)
        table = jnp.where(from_peer[:, None, None], got, table)
        step += 1
    stats += [window_stats(h, *window) for h in heads[len(stats) :]]

    def header_part(at, table):
        return header_grads(heads[at], links, queries, out_grad, table, stats[at])

    def window_part(stage, at, fin, carried, part=None):
        return window_grads(stage, heads[at], *window, *fin, part, carried)

    other_side = xor_permute(table, 2)
    *fin0, own_sum = header_part(0, table)
    other_side, own_sum = barrier((other_side, own_sum))
    other_core = xor_permute(jnp.stack([other_side, table]), 1)
    *fin1, side_sum = header_part(1, other_side)
    arrived = [xor_permute(side_sum, 2)]
    *fin2, far_sum = header_part(2, other_core[0])
    arrived.append(xor_permute(far_sum, 3))
    *fin3, core_sum = header_part(3, other_core[1])
    arrived.append(xor_permute(core_sum, 1))

    fins = [fin0, fin1, fin2, fin3]
    fins, core_sum = barrier((fins, core_sum))
    query_grad, back, dk, dv = window_part(ALL, 0, fins[0], {})
    own_parts = [None]
    total = own_sum.astype(jnp.float32)
    arrived, query_grad = barrier((arrived, query_grad))
    for x in arrived:
        total = total + x.astype(jnp.float32)
    step -= 1
    sent, query_grad = barrier((total.astype(jnp.bfloat16), query_grad))
    got = xor_permute(sent, 4 << step)
    for at in range(1, KEY_VALUE_HEADS):
        query_grad, back, part = window_part(FIRST, at, fins[at], {0: query_grad, 1: back})
        own_parts.append(part)
    back = shifted(back, -1)
    query_grad, dk, dv = window_part(REST, 1, fins[1], dict(enumerate((query_grad, dk, dv))), own_parts[1])
    got, query_grad = barrier((got, query_grad))
    total = total + got.astype(jnp.float32)
    while step > 1:
        step -= 1
        total = total + xor_permute(total.astype(jnp.bfloat16), 4 << step).astype(jnp.float32)
    sent, query_grad = barrier((total.astype(jnp.bfloat16), query_grad))
    got = xor_permute(sent, 4)
    query_grad, dk, dv = window_part(REST, 2, fins[2], dict(enumerate((query_grad, dk, dv))), own_parts[2])
    got, back, query_grad = barrier((got, back, query_grad))
    total = total + got.astype(jnp.float32)

    group = me ^ jnp.arange(4, dtype=jnp.int32)
    wanted = owners[None, :] == group[:, None]
    owned = jnp.sum(jnp.where(wanted[:, :, None, None], total[None], 0.0), axis=1).astype(jnp.bfloat16)
    owned, query_grad = barrier((owned, query_grad))
    side = xor_permute(owned[2:], 2)
    query_grad, dk, dv = window_part(REST, 3, fins[3], dict(enumerate((query_grad, dk, dv))), own_parts[3])
    side, dk = barrier((side, dk))
    far = xor_permute(jnp.stack([owned[1], side[1]]), 1)
    back = back.astype(jnp.float32)
    parts = (owned[0], far[0], side[0], far[1])
    offset = jnp.sum(jnp.where(owners == me, header_blocks % blocks + 1, 0)) - 1

    def summed(grad, returned, columns):
        own = []
        for head in range(KEY_VALUE_HEADS):
            x = parts[head ^ 3]
            for other in range(3):
                x = jnp.where(low == other, parts[head ^ other], x)
            own.append(x[:, columns].astype(jnp.float32))
        own = jnp.concatenate(own, axis=1)
        pieces = []
        for block in range(blocks):
            piece = grad[block * BLK : (block + 1) * BLK]
            at = block * BLK - (rows - WIN)
            if at >= 0:
                piece = piece + returned[at : at + BLK]
            pieces.append(piece + jnp.where(offset == block, own, 0.0))
        return jnp.concatenate(pieces, axis=0)

    dk = summed(dk, back[0], slice(0, HEAD_SIZE))
    dv = summed(dv, back[1], slice(HEAD_SIZE, 2 * HEAD_SIZE))
    return query_grad, dk, dv


def solution(mesh):
    rows = P(("groups", "ctx"), None)
    return jax.shard_map(
        body,
        mesh=mesh,
        in_specs=(rows, rows, rows, rows, rows, P("groups")),
        out_specs=(rows, rows, rows),
        check_vma=False,
    )
```
